32 devices in a mesh: grp: 4 (over y, core), dp: 8 (over z, x).
Axes of the slice: x: 2, y: 2, z: 4, core: 2. Of those that a mesh axis runs over, the one named last changes fastest.
Arguments:
- image_in: bfloat16 [256, 14, 14, 2048], P(('grp', 'dp')), may hold values from -16 to 16
- slot_mask: int32 [256], P(('grp', 'dp')), may hold values from 0 to 1, as said below
- conv_reduce: bfloat16 [2048, 1024], replicated, may hold values from -0.125 to 0.125
- gain_reduce: bfloat16 [1024], replicated, may hold values from 0.5 to 1.5
- bias_reduce: bfloat16 [1024], replicated, may hold values from -2 to 2
- conv_group: bfloat16 [3, 3, 32, 1024], P(None, None, None, 'grp'), may hold values from -0.375 to 0.375
- gain_group: bfloat16 [1024], P('grp'), may hold values from 0.5 to 1.5
- bias_group: bfloat16 [1024], P('grp'), may hold values from -2 to 2
- conv_expand: bfloat16 [1024, 2048], replicated, may hold values from -0.1875 to 0.1875
- gain_expand: bfloat16 [2048], replicated, may hold values from 0.5 to 1.5
- bias_expand: bfloat16 [2048], replicated, may hold values from -2 to 2
- out_grad: bfloat16 [256, 14, 14, 2048], P(('grp', 'dp')), may hold values from -8 to 8
Outputs:
- block_out: bfloat16 [256, 14, 14, 2048], P(('grp', 'dp'))
- image_grad: bfloat16 [256, 14, 14, 2048], P(('grp', 'dp'))
- reduce_wgrad: float32 [2048, 1024], replicated
- gain_reduce_grad: float32 [1024], replicated
- bias_reduce_grad: float32 [1024], replicated
- group_wgrad: float32 [3, 3, 32, 1024], P(None, None, None, 'grp')
- gain_group_grad: float32 [1024], P('grp')
- bias_group_grad: float32 [1024], P('grp')
- expand_wgrad: float32 [1024, 2048], replicated
- gain_expand_grad: float32 [2048], replicated
- bias_expand_grad: float32 [2048], replicated
The draws below stay inside these ranges and needn't reach their ends.
Inputs may be any that keep to these rules, and one draw needn't show every extreme that they name: `slot_mask`: at least one slot is valid.
All inputs are finite; a program needn't handle non-finite values.
Results may differ from the reference program's by a relative error of at most 0.012.
Values may be sent and summed in bfloat16 or wider, within the bound.
A program may use at most 320 MiB of HBM per device.

```python
import jax
import jax.numpy as jnp
from jax import lax

C = 2048
WIDTH = 1024
GROUPS = 32
SIDE = 14
GROUP_WIDTH = 32
IMAGES = 256


def rising_scale(factor):
    image_index = jnp.arange(IMAGES, dtype=jnp.float32)
    return jnp.exp(jnp.log(factor) * image_index / max(IMAGES - 1, 1))


def draw_image_in(key, part):
    key = jax.random.fold_in(key, 11)
    noise_key, channel_key = jax.random.split(key, 2)
    full_shape = (IMAGES, SIDE, SIDE, C)
    values = jax.random.normal(noise_key, full_shape, jnp.float32)
    row_scale = rising_scale(3.0)
    channel_scale = jnp.exp(jax.random.uniform(channel_key, (C,), jnp.float32, jnp.log(0.3), jnp.log(3.0)))
    scaled_field = 0.5 * values * channel_scale * row_scale.reshape(IMAGES, 1, 1, 1)
    return jnp.clip(scaled_field, -16.0, 16.0).astype(jnp.bfloat16)


def draw_out_grad(key, part):
    key = jax.random.fold_in(key, 13)
    full_shape = (IMAGES, SIDE, SIDE, C)
    values = jax.random.normal(key, full_shape, jnp.float32)
    row_scale = rising_scale(3.0)
    scaled_field = values * row_scale.reshape(IMAGES, 1, 1, 1)
    return jnp.clip(scaled_field, -8.0, 8.0).astype(jnp.bfloat16)


def draw_slot_mask(key, part):
    key = jax.random.fold_in(key, 5)
    pick_key, coin_key = jax.random.split(key)
    valid = jax.random.randint(coin_key, (IMAGES,), 0, 10) < 9
    forced = jnp.arange(IMAGES, dtype=jnp.int32) == jax.random.randint(pick_key, (), 0, IMAGES)
    return jnp.where(valid | forced, 1, 0).astype(jnp.int32)


def block_levels(own_key, dims, pieces, smallest, top_value):
    level, own = 1.0, jax.random.fold_in(own_key, 6)
    for axis_at, shards_of in pieces:
        heights = jnp.exp(jax.random.uniform(jax.random.fold_in(own, axis_at), (shards_of,), jnp.float32, smallest / len(pieces), top_value / len(pieces)))
        level = level * jnp.repeat(heights, dims[axis_at] // shards_of).reshape([-1 if axis == axis_at else 1 for axis in range(len(dims))])
    return level


def bell_draw(stream_key, shape, scale, most, pieces=(), held_as=jnp.bfloat16):
    level = block_levels(stream_key, shape, pieces, -0.22, 0.18) if pieces else 1.0
    array = jax.random.normal(stream_key, shape, jnp.float32) * scale * level
    return jnp.minimum(jnp.maximum(array, -most), most).astype(held_as)


def setup_inputs(seed: int = 0) -> dict:
    arg_keys = jax.random.split(jax.random.key(seed), 13)
    image_in = draw_image_in(jax.random.fold_in(arg_keys[12], 71), 0)
    slot_mask = draw_slot_mask(jax.random.fold_in(arg_keys[12], 71), 0)
    conv_reduce = bell_draw(arg_keys[2], (C, WIDTH), C ** -0.5, 0.125)
    gain_reduce = jnp.clip(jax.random.uniform(arg_keys[3], (WIDTH,), jnp.float32, 0.5, 1.5), 0.5, 1.5).astype(jnp.bfloat16)
    bias_reduce = bell_draw(arg_keys[4], (WIDTH,), 0.5, 2.0)
    conv_group = bell_draw(arg_keys[5], (3, 3, GROUP_WIDTH, WIDTH), (9 * GROUP_WIDTH) ** -0.5, 0.375, ((3, 4),))
    gain_group = jnp.clip(0.5 + 1.0 * jax.random.uniform(arg_keys[6], (WIDTH,), jnp.float32) ** block_levels(arg_keys[6], (WIDTH,), ((0, 4),), -0.2, 0.2), 0.5, 1.5).astype(jnp.bfloat16)
    bias_group = bell_draw(arg_keys[7], (WIDTH,), 0.5, 2.0, ((0, 4),))
    conv_expand = bell_draw(arg_keys[8], (WIDTH, C), WIDTH ** -0.5, 0.1875)
    gain_expand = jnp.clip(jax.random.uniform(arg_keys[9], (C,), jnp.float32, 0.5, 1.5), 0.5, 1.5).astype(jnp.bfloat16)
    bias_expand = bell_draw(arg_keys[10], (C,), 0.5, 2.0)
    out_grad = draw_out_grad(jax.random.fold_in(arg_keys[12], 71), 0)
    return dict(image_in=image_in, slot_mask=slot_mask, conv_reduce=conv_reduce, gain_reduce=gain_reduce, bias_reduce=bias_reduce, conv_group=conv_group, gain_group=gain_group, bias_group=bias_group, conv_expand=conv_expand, gain_expand=gain_expand, bias_expand=bias_expand, out_grad=out_grad)


EPS = 1e-05

@jax.custom_vjp
def low(v):
    return lax.optimization_barrier(v.astype(jnp.bfloat16)).astype(jnp.float32)

@jax.custom_vjp
def low_back(v):
    return v

def low_keep(v):
    return (low(v), None)

def low_pass(kept, grad):
    return (grad,)

def back_keep(v):
    return (v, None)

def back_low(kept, grad):
    return (low(grad),)
low.defvjp(low_keep, low_pass)
low_back.defvjp(back_keep, back_low)

def batch_norm(values, weight_mask, pixel_count, gain, shift):
    average = lax.optimization_barrier(jnp.sum(values * weight_mask, axis=(0, 1, 2))) / pixel_count
    centred = values - average
    spread = lax.optimization_barrier(jnp.sum(weight_mask * centred * centred, axis=(0, 1, 2))) / pixel_count
    return centred * lax.rsqrt(spread + EPS) * gain + shift

def forward(image_f, reduce_f, gain_reduce, bias_reduce, group_f, gain_group, bias_group, expand_f, gain_expand, bias_expand, weight_mask, pixel_count):
    reduced = low_back(jnp.einsum('nhwc,cd->nhwd', low(image_f), low(reduce_f), precision=lax.Precision.HIGHEST))
    hidden_one = low_back(low(jax.nn.silu(batch_norm(reduced, weight_mask, pixel_count, gain_reduce, bias_reduce))))
    mixed_out = low_back(lax.conv_general_dilated(hidden_one, low(group_f), (1, 1), 'SAME', dimension_numbers=('NHWC', 'HWIO', 'NHWC'), feature_group_count=GROUPS, precision=lax.Precision.HIGHEST))
    hidden_two = low_back(low(jax.nn.silu(batch_norm(mixed_out, weight_mask, pixel_count, gain_group, bias_group))))
    expanded = low_back(jnp.einsum('nhwd,dc->nhwc', hidden_two, low(expand_f), precision=lax.Precision.HIGHEST))
    summed = batch_norm(expanded, weight_mask, pixel_count, gain_expand, bias_expand) + image_f
    return weight_mask * jax.nn.silu(summed)

def reference(image_in, slot_mask, conv_reduce, gain_reduce, bias_reduce, conv_group, gain_group, bias_group, conv_expand, gain_expand, bias_expand, out_grad):
    weight_mask = slot_mask.astype(jnp.float32).reshape(-1, 1, 1, 1)
    pixel_count = jnp.sum(slot_mask).astype(jnp.float32) * (SIDE * SIDE)

    def block(image_f, reduce_f, gain_a, bias_a, group_f, gain_b, bias_b, expand_f, gain_c, bias_c):
        return forward(image_f, reduce_f, gain_a, bias_a, group_f, gain_b, bias_b, expand_f, gain_c, bias_c, weight_mask, pixel_count)
    result, pullback = jax.vjp(block, image_in.astype(jnp.float32), conv_reduce.astype(jnp.float32), gain_reduce.astype(jnp.float32), bias_reduce.astype(jnp.float32), conv_group.astype(jnp.float32), gain_group.astype(jnp.float32), bias_group.astype(jnp.float32), conv_expand.astype(jnp.float32), gain_expand.astype(jnp.float32), bias_expand.astype(jnp.float32))
    grads = pullback(out_grad.astype(jnp.float32))
    return (result.astype(jnp.bfloat16), grads[0].astype(jnp.bfloat16), grads[1], grads[2], grads[3], grads[4], grads[5], grads[6], grads[7], grads[8], grads[9])
```

```python
import functools

import jax
import jax.numpy as jnp
from jax import lax
from jax.experimental import pallas as pl
from jax.experimental.pallas import tpu as pltpu
from jax.sharding import PartitionSpec as P

EPS = 1e-05
BF = jnp.bfloat16
F32 = jnp.float32
MESH = pl.DeviceIdType.MESH
CB = 128
VMEM_LIMIT = 61952 * 1024


def aligned(index, size):
    return pl.ds(pl.multiple_of(index * size, size), size)


def sigmoid(values):
    return 0.5 * jnp.tanh(0.5 * values) + 0.5


def fold(values, images):
    rows, cols = values.shape
    return jnp.sum(values.reshape(rows // images, images, cols), axis=0)


def down(values):
    return jnp.sum(values, axis=0, keepdims=True)


def spread_rows(values, row):
    rows, cols = values.shape
    images = row.shape[0]
    return (values.reshape(rows // images, images, cols) * wide(row, cols)[None]).reshape(rows, cols)


class Links:
    def __init__(self, grp, dp):
        self.grp, self.dp = grp, dp
        self.count = grp * dp
        self.g, self.d = lax.axis_index("grp"), lax.axis_index("dp")
        self.me = self.g * dp + self.d

    def peer(self, step):
        target = lax.rem(self.me + step, self.count)
        return (target // self.dp, lax.rem(target, self.dp))

    def greet(self):
        barrier = pltpu.get_barrier_semaphore()

        @pl.loop(1, self.count)
        def _(step):
            pl.semaphore_signal(barrier, inc=1, device_id=self.peer(step), device_id_type=MESH)

    def greeted(self):
        pl.semaphore_wait(pltpu.get_barrier_semaphore(), self.count - 1)

    def send(self, buf, send_sem, recv_sem):
        @pl.loop(1, self.count)
        def _(step):
            pltpu.make_async_remote_copy(
                src_ref=buf.at[self.me],
                dst_ref=buf.at[self.me],
                send_sem=send_sem,
                recv_sem=recv_sem,
                device_id=self.peer(step),
                device_id_type=MESH,
            ).start()

    def wait(self, buf, send_sem, recv_sem):
        others = buf.at[pl.ds(0, self.count - 1)]
        copy = pltpu.make_async_remote_copy(
            src_ref=others,
            dst_ref=others,
            send_sem=send_sem,
            recv_sem=recv_sem,
            device_id=self.peer(1),
            device_id_type=MESH,
        )
        copy.wait_recv()
        copy.wait_send()


def wide(row, cols):
    return jnp.concatenate([row] * (cols // 128), axis=-1)


def row_weights(mask_ref, images):
    at = lax.broadcasted_iota(jnp.int32, (images, 128), 0)
    column = jnp.zeros((images, 128), F32)
    count = jnp.float32(0.0)
    for i in range(images):
        value = mask_ref[i].astype(F32)
        column = jnp.where(at == i, value, column)
        count = count + value
    return column, count


def merge_stats(buf, counts, cols):
    each = wide(counts, cols)
    total = jnp.sum(each, axis=0)
    parts = buf[...]
    means, squares = parts[:, 0:1], parts[:, 1:2]
    average = jnp.sum(each * means, axis=0) / total
    gap = means - average
    spread = jnp.sum(squares + each * gap * gap, axis=0) / total
    return average, lax.rsqrt(spread + EPS)


def dense_taps(shard):
    group = 32
    row = lax.broadcasted_iota(jnp.int32, (CB, CB), 0) // group
    col = lax.broadcasted_iota(jnp.int32, (CB, CB), 1) // group
    keep = row == col
    zero = jnp.zeros((CB, CB), BF)

    def block(row_tap, col_tap):
        start = (row_tap * 3 + col_tap) * group
        tile = shard(start, group).astype(F32)
        full = jnp.concatenate([tile] * (CB // group), axis=0)
        return jnp.where(keep, full, 0.0).astype(BF)

    return block, zero


def shifted(values, images):
    edge = jnp.zeros((images, values.shape[1]), F32)
    return (
        jnp.concatenate([edge, values[:-images]], axis=0),
        jnp.concatenate([values[images:], edge], axis=0),
    )


def local_stats(field, cols, mean_of, rows, chunk, images, row, inverse, width):
    mean = down(mean_of * wide(row, width)) * wide(inverse, width)

    def body(k, acc):
        gap = field[aligned(k, chunk), cols] - mean
        return acc + fold(gap * gap, images)

    squares = lax.fori_loop(0, rows // chunk, body, jnp.zeros((images, width), F32))
    return mean, down(squares * wide(row, width))


def ka_kernel(
    dims,
    x_hbm,
    wr_hbm,
    wg_hbm,
    par_ref,
    mask_ref,
    red_hbm,
    mixed_hbm,
    p1_ref,
    p2_ref,
    wgall_hbm,
    xv,
    wr,
    red,
    mixed,
    wgall,
    taps,
    hbuf,
    cnt,
    ex1,
    ex2,
    load_sem,
    store_sem,
    gather_sem,
    cnt_sem,
    ex1_sem,
    ex2_sem,
):
    n, side, C, W, grp, dp, cg = dims
    rows = side * side * n
    line = side * n
    half = W // 2
    tile = rows // 2
    links = Links(grp, dp)
    links.greet()
    w_loads = [
        pltpu.make_async_copy(
            wr_hbm.at[:, pl.ds(h * half, half)], wr.at[:, pl.ds(h * half, half)], load_sem.at[h]
        )
        for h in range(2)
    ]
    x_loads = [
        pltpu.make_async_copy(
            x_hbm.at[pl.ds(h * tile, tile), :], xv.at[pl.ds(h * tile, tile), :], load_sem.at[2 + h]
        )
        for h in range(2)
    ]
    w_loads[0].start()
    x_loads[0].start()
    x_loads[1].start()
    w_loads[1].start()
    own = pltpu.make_async_copy(wg_hbm, wgall.at[links.g], load_sem.at[4])
    own.start()

    row, valid = row_weights(mask_ref, n)
    local = jnp.full((1, 128), 1.0, F32) * (valid * float(side * side))
    cnt[links.me] = local
    inverse = 1.0 / jnp.maximum(local, 1.0)
    hbuf[...] = jnp.zeros(hbuf.shape, BF)
    links.greeted()
    links.send(cnt, cnt_sem.at[0], cnt_sem.at[1])
    gathers = []
    for k in range(1, grp):
        copy = pltpu.make_async_remote_copy(
            src_ref=wg_hbm,
            dst_ref=wgall.at[links.g],
            send_sem=gather_sem.at[0, k - 1],
            recv_sem=gather_sem.at[1, k - 1],
            device_id=(lax.rem(links.g + k, grp), links.d),
            device_id_type=MESH,
        )
        copy.start()
        gathers.append(copy)

    for h in range(2):
        w_loads[h].wait()
        cols = pl.ds(h * half, half)
        total = jnp.zeros((n, half), F32)
        for t in range(2):
            if h == 0:
                x_loads[t].wait()
            at = pl.ds(t * tile, tile)
            out = jnp.dot(xv[at, :], wr[:, cols], preferred_element_type=F32)
            red[at, cols] = out
            total += fold(out, n)
        mean, squares = local_stats(red, cols, total, rows, line, n, row, inverse, half)
        ex1[h, links.me, 0:1, :] = mean
        ex1[h, links.me, 1:2, :] = squares
        if h == 0:
            links.wait(cnt, cnt_sem.at[0], cnt_sem.at[1])
        links.send(ex1.at[h], ex1_sem.at[0, h], ex1_sem.at[1, h])
    red_store = pltpu.make_async_copy(red, red_hbm, store_sem.at[0])
    red_store.start()

    own.wait()
    for copy in gathers:
        copy.wait()
    store_wg = pltpu.make_async_copy(wgall, wgall_hbm, store_sem.at[1])
    store_wg.start()
    blocks = W // CB
    per_shard = cg // CB

    @pl.loop(0, blocks)
    def _(b):
        shard_at, lane = b // per_shard, aligned(lax.rem(b, per_shard), CB)
        block, zero = dense_taps(lambda start, size: wgall[shard_at, pl.ds(start, size), lane])
        for dx in range(3):
            taps[b, pl.ds(dx * CB, CB), 0:CB] = block(0, dx)
            taps[b, pl.ds(dx * CB, CB), CB : 2 * CB] = zero
            taps[b, pl.ds((3 + dx) * CB, CB), 0:CB] = block(1, dx)
            taps[b, pl.ds((3 + dx) * CB, CB), CB : 2 * CB] = block(2, dx)

    for h in range(2):
        links.wait(ex1.at[h], ex1_sem.at[0, h], ex1_sem.at[1, h])
        cols = pl.ds(h * half, half)
        average, scale = merge_stats(ex1.at[h], cnt[...], half)
        p1_ref[0:1, cols] = average
        p1_ref[1:2, cols] = scale

        @pl.loop(h * blocks // 2, (h + 1) * blocks // 2)
        def _(b):
            lanes = aligned(b, CB)
            mean, rstd = p1_ref[0:1, lanes], p1_ref[1:2, lanes]
            gain, shift = par_ref[0:1, lanes], par_ref[1:2, lanes]

            @pl.loop(0, side)
            def _(r):
                act = (red[aligned(r, line), lanes] - mean) * rstd * gain + shift
                hidden = act * sigmoid(act)
                left, right = shifted(hidden, n)
                to = aligned(r + 1, line)
                hbuf[to, 0:CB] = left.astype(BF)
                hbuf[to, CB : 2 * CB] = hidden.astype(BF)
                hbuf[to, 2 * CB : 3 * CB] = right.astype(BF)

            lhs = jnp.concatenate([hbuf[0 : rows + line, :], hbuf[line : rows + 2 * line, :]], axis=1)
            out = jnp.dot(lhs, taps[b], preferred_element_type=F32)
            field = out[0:rows, 0:CB] + out[line : line + rows, CB:]
            mixed[:, lanes] = field
            mean, squares = local_stats(
                mixed, lanes, fold(field, n), rows, line, n, row, inverse, CB
            )
            inner = aligned(lax.rem(b, blocks // 2), CB)
            ex2[h, links.me, 0:1, inner] = mean
            ex2[h, links.me, 1:2, inner] = squares

        links.send(ex2.at[h], ex2_sem.at[0, h], ex2_sem.at[1, h])
        pltpu.make_async_copy(mixed.at[:, cols], mixed_hbm.at[:, cols], store_sem.at[2 + h]).start()

    count = jnp.sum(wide(cnt[...], W), axis=0)
    p1_ref[2:3, :] = count
    p2_ref[2:3, :] = count
    extra = jnp.concatenate(
        [wgall[k, pl.ds(9 * 32, 16), :].astype(F32) for k in range(grp)], axis=1
    )
    p2_ref[3:5, :] = extra[0:2]
    p1_ref[3:5, :] = par_ref[0:2, :]
    for h in range(2):
        links.wait(ex2.at[h], ex2_sem.at[0, h], ex2_sem.at[1, h])
        cols = pl.ds(h * half, half)
        average, scale = merge_stats(ex2.at[h], cnt[...], half)
        p2_ref[0:1, cols] = average
        p2_ref[1:2, cols] = scale
    red_store.wait()
    store_wg.wait()
    for h in range(2):
        cols = pl.ds(h * half, half)
        pltpu.make_async_copy(mixed.at[:, cols], mixed_hbm.at[:, cols], store_sem.at[2 + h]).wait()


def kb_kernel(
    dims,
    mixed_hbm,
    p2_ref,
    we_hbm,
    x_hbm,
    dout_hbm,
    par_ref,
    mask_ref,
    out_hbm,
    pre_hbm,
    h2g_hbm,
    ewg_hbm,
    sums3_ref,
    sums2_ref,
    mixed,
    we,
    h2,
    expd,
    xe,
    dout,
    n3,
    h2g,
    stat3,
    cnt,
    ex3,
    ex4,
    load_sem,
    store_sem,
    cnt_sem,
    ex3_sem,
    ex4_sem,
    ex5_sem,
):
    n, side, C, W, grp, dp, cg = dims
    rows = side * side * n
    line = side * n
    half = W // 2
    tile = rows // 2
    links = Links(grp, dp)
    links.greet()
    part_cols = 512
    parts = C // part_cols
    pieces = 7
    piece = rows // pieces
    m_loads = [
        pltpu.make_async_copy(
            mixed_hbm.at[pl.ds(k * piece, piece), :],
            mixed.at[pl.ds(k * piece, piece), :],
            load_sem.at[k],
        )
        for k in range(pieces)
    ]
    for copy in m_loads:
        copy.start()
    we_load = pltpu.make_async_copy(we_hbm, we, load_sem.at[pieces])
    we_load.start()
    x_load = pltpu.make_async_copy(x_hbm, xe, load_sem.at[pieces + 1])
    x_load.start()
    d_load = pltpu.make_async_copy(dout_hbm, dout, load_sem.at[pieces + 2])
    d_load.start()
    row, valid = row_weights(mask_ref, n)
    local = jnp.full((1, 128), 1.0, F32) * (valid * float(side * side))
    cnt[links.me] = local
    inverse = 1.0 / jnp.maximum(local, 1.0)
    links.greeted()
    links.send(cnt, cnt_sem.at[0], cnt_sem.at[1])

    step = 256
    lines = rows // line
    for k in range(pieces):
        m_loads[k].wait()

        @pl.loop(k * lines // pieces, (k + 1) * lines // pieces)
        def _(r):
            at = aligned(r, line)
            for q in range(W // step):
                lanes = pl.ds(q * step, step)
                normed = (mixed[at, lanes] - p2_ref[0:1, lanes]) * p2_ref[1:2, lanes]
                act = normed * p2_ref[3:4, lanes] + p2_ref[4:5, lanes]
                h2[at, lanes] = (act * sigmoid(act)).astype(BF)

    we_load.wait()
    links.wait(cnt, cnt_sem.at[0], cnt_sem.at[1])
    for part in range(parts):
        cols = pl.ds(part * part_cols, part_cols)
        total = jnp.zeros((n, part_cols), F32)
        for t in range(2):
            at = pl.ds(t * tile, tile)
            out = jnp.dot(h2[at, :], we[:, cols], preferred_element_type=F32)
            expd[at, cols] = out
            total += fold(out, n)
        mean, squares = local_stats(expd, cols, total, rows, line, n, row, inverse, part_cols)
        ex3[part, links.me, 0:1, :] = mean
        ex3[part, links.me, 1:2, :] = squares
        links.send(ex3.at[part], ex3_sem.at[0, part], ex3_sem.at[1, part])

    x_load.wait()
    d_load.wait()
    step = 128
    for part in range(parts):
        cols = pl.ds(part * part_cols, part_cols)
        links.wait(ex3.at[part], ex3_sem.at[0, part], ex3_sem.at[1, part])
        average, scale = merge_stats(ex3.at[part], cnt[...], part_cols)
        stat3[0:1, cols] = average
        stat3[1:2, cols] = scale

        @pl.loop(0, part_cols // step)
        def _(q):
            lanes = pl.ds(pl.multiple_of(part * part_cols + q * step, step), step)
            mean, rstd = stat3[0:1, lanes], stat3[1:2, lanes]
            gain, shift = par_ref[0:1, lanes], par_ref[1:2, lanes]

            def body(r, sums):
                at = aligned(r, line)
                normed = (expd[at, lanes] - mean) * rstd
                summed = normed * gain + shift + xe[at, lanes].astype(F32)
                sig = sigmoid(summed)
                silu = summed * sig
                grad = spread_rows(dout[at, lanes].astype(F32), row) * (sig + silu * (1.0 - sig))
                dout[at, lanes] = spread_rows(silu, row).astype(BF)
                expd[at, lanes] = grad
                n3[at, lanes] = normed.astype(BF)
                return sums[0] + fold(grad * normed, n), sums[1] + fold(grad, n)

            zeros = jnp.zeros((n, step), F32)
            gain_sum, shift_sum = lax.fori_loop(0, lines, body, (zeros, zeros))
            inner = aligned(q, step)
            ex4[part, links.me, 0:1, inner] = down(gain_sum)
            ex4[part, links.me, 1:2, inner] = down(shift_sum)

        links.send(ex4.at[part], ex4_sem.at[0, part], ex4_sem.at[1, part])
    out_store = pltpu.make_async_copy(dout, out_hbm, store_sem.at[0])
    out_store.start()
    pre_store = pltpu.make_async_copy(expd, pre_hbm, store_sem.at[1])
    pre_store.start()

    total = jnp.sum(wide(cnt[...], part_cols), axis=0)
    for part in range(parts):
        cols = pl.ds(part * part_cols, part_cols)
        links.wait(ex4.at[part], ex4_sem.at[0, part], ex4_sem.at[1, part])
        sums = jnp.sum(ex4[part], axis=0)
        sums3_ref[0:2, cols] = sums
        stat3[2:3, cols] = sums[0:1] / total
        stat3[3:4, cols] = sums[1:2] / total
        stat3[4:5, cols] = par_ref[0:1, cols] * stat3[1:2, cols]

        @pl.loop(0, lines)
        def _(r):
            at = aligned(r, line)
            for q in range(part_cols // step):
                lanes = pl.ds(part * part_cols + q * step, step)
                off = stat3[3:4, lanes] + n3[at, lanes].astype(F32) * stat3[2:3, lanes]
                value = stat3[4:5, lanes] * (expd[at, lanes] - spread_rows(off, row))
                xe[at, lanes] = value.astype(BF)

    ex5 = ex3
    for h in range(2):
        cols = pl.ds(h * half, half)
        for t in range(2):
            at = pl.ds(t * tile, tile)
            h2g[at, cols] = lax.dot_general(
                xe[at, :], we[cols, :], (((1,), (1,)), ((), ())), preferred_element_type=F32
            ).astype(BF)

        @pl.loop(0, half // step)
        def _(q):
            lanes = pl.ds(pl.multiple_of(h * half + q * step, step), step)
            mean, rstd = p2_ref[0:1, lanes], p2_ref[1:2, lanes]
            gain, shift = p2_ref[3:4, lanes], p2_ref[4:5, lanes]

            def body(r, sums):
                at = aligned(r, line)
                normed = (mixed[at, lanes] - mean) * rstd
                act = normed * gain + shift
                sig = sigmoid(act)
                grad = h2g[at, lanes].astype(F32) * (sig + act * sig * (1.0 - sig))
                return sums[0] + fold(grad * normed, n), sums[1] + fold(grad, n)

            zeros = jnp.zeros((n, step), F32)
            gain_sum, shift_sum = lax.fori_loop(0, lines, body, (zeros, zeros))
            inner = aligned(q, step)
            ex5[h, links.me, 0:1, inner] = down(gain_sum)
            ex5[h, links.me, 1:2, inner] = down(shift_sum)

        links.send(ex5.at[h], ex5_sem.at[0, h], ex5_sem.at[1, h])
    h2g_store = pltpu.make_async_copy(h2g, h2g_hbm, store_sem.at[2])
    h2g_store.start()

    ewg = we
    for part in range(parts):
        cols = pl.ds(part * part_cols, part_cols)
        ewg[:, cols] = lax.dot_general(
            h2[...], xe[:, cols], (((0,), (0,)), ((), ())), preferred_element_type=F32
        ).astype(BF)
    ewg_store = pltpu.make_async_copy(ewg, ewg_hbm, store_sem.at[3])
    ewg_store.start()
    for h in range(2):
        links.wait(ex5.at[h], ex5_sem.at[0, h], ex5_sem.at[1, h])
        sums2_ref[0:2, pl.ds(h * half, half)] = jnp.sum(ex5[h], axis=0)
    out_store.wait()
    pre_store.wait()
    h2g_store.wait()
    ewg_store.wait()


def kc_kernel(
    dims,
    h2g_hbm,
    mixed_hbm,
    red_hbm,
    p1_ref,
    p2_ref,
    sums2_ref,
    wgall_ref,
    x_hbm,
    wr_hbm,
    pre_hbm,
    mask_ref,
    ig_hbm,
    rwg_hbm,
    gwg_ref,
    sums1_ref,
    h2g,
    mixed,
    red,
    xv,
    wr,
    pre,
    rwg,
    taps,
    dbuf,
    hbuf,
    coef,
    ex6,
    block_sem,
    load_sem,
    store_sem,
    ex6_sem,
):
    n, side, C, W, grp, dp, cg = dims
    rows = side * side * n
    line = side * n
    half = W // 2
    tile = rows // 2
    blocks = W // CB
    per_shard = cg // CB
    links = Links(grp, dp)
    links.greet()

    def block_loads(b):
        lanes = aligned(b, CB)
        return [
            pltpu.make_async_copy(src.at[:, lanes], dst.at[:, lanes], block_sem.at[k, b])
            for k, (src, dst) in enumerate(((h2g_hbm, h2g), (mixed_hbm, mixed), (red_hbm, red)))
        ]

    @pl.loop(0, blocks)
    def _(b):
        for copy in block_loads(b):
            copy.start()

    loads = [
        pltpu.make_async_copy(src, dst, load_sem.at[k])
        for k, (src, dst) in enumerate(((x_hbm, xv), (wr_hbm, wr), (pre_hbm, pre)))
    ]
    for copy in loads:
        copy.start()
    row, valid = row_weights(mask_ref, n)
    dbuf[...] = jnp.zeros(dbuf.shape, BF)
    hbuf[...] = jnp.zeros(hbuf.shape, BF)
    total = p2_ref[2:3, :]
    coef[0:1, :] = sums2_ref[0:1, :] / total
    coef[1:2, :] = sums2_ref[1:2, :] / total
    coef[2:3, :] = p2_ref[3:4, :] * p2_ref[1:2, :]

    @pl.loop(0, blocks)
    def _(b):
        shard_at, lane = b // per_shard, aligned(lax.rem(b, per_shard), CB)
        block, zero = dense_taps(lambda start, size: wgall_ref[shard_at, pl.ds(start, size), lane])
        for dx in range(3):
            taps[b, 0:CB, pl.ds(dx * CB, CB)] = block(2, 2 - dx)
            taps[b, CB : 2 * CB, pl.ds(dx * CB, CB)] = zero
            taps[b, 0:CB, pl.ds((3 + dx) * CB, CB)] = block(1, 2 - dx)
            taps[b, CB : 2 * CB, pl.ds((3 + dx) * CB, CB)] = block(0, 2 - dx)

    links.greeted()
    group = 32
    keep = (
        lax.broadcasted_iota(jnp.int32, (CB, CB), 0) // group
        == lax.broadcasted_iota(jnp.int32, (CB, CB), 1) // group
    )
    for h in range(2):

        @pl.loop(h * blocks // 2, (h + 1) * blocks // 2)
        def _(b):
            for copy in block_loads(b):
                copy.wait()
            lanes = aligned(b, CB)

            @pl.loop(0, side)
            def _(r):
                at = aligned(r, line)
                normed = (mixed[at, lanes] - p2_ref[0:1, lanes]) * p2_ref[1:2, lanes]
                act = normed * p2_ref[3:4, lanes] + p2_ref[4:5, lanes]
                sig = sigmoid(act)
                grad = h2g[at, lanes].astype(F32) * (sig + act * sig * (1.0 - sig))
                off = coef[1:2, lanes] + normed * coef[0:1, lanes]
                grad = coef[2:3, lanes] * (grad - spread_rows(off, row))
                left, right = shifted(grad, n)
                to = aligned(r + 1, line)
                dbuf[to, 0:CB] = left.astype(BF)
                dbuf[to, CB : 2 * CB] = grad.astype(BF)
                dbuf[to, 2 * CB : 3 * CB] = right.astype(BF)

            lhs = jnp.concatenate([dbuf[0 : rows + line, :], dbuf[line : rows + 2 * line, :]], axis=1)
            out = lax.dot_general(
                lhs, taps[b], (((1,), (1,)), ((), ())), preferred_element_type=F32
            )
            mixed[:, lanes] = out[0:rows, 0:CB] + out[line : line + rows, CB:]
            mean, rstd = p1_ref[0:1, lanes], p1_ref[1:2, lanes]
            gain, shift = p1_ref[3:4, lanes], p1_ref[4:5, lanes]

            def body(r, sums):
                at = aligned(r, line)
                normed = (red[at, lanes] - mean) * rstd
                act = normed * gain + shift
                sig = sigmoid(act)
                silu = act * sig
                hbuf[aligned(r + 1, line), :] = silu.astype(BF)
                grad = mixed[at, lanes].astype(BF).astype(F32) * (sig + silu * (1.0 - sig))
                mixed[at, lanes] = grad
                return sums[0] + fold(grad * normed, n), sums[1] + fold(grad, n)

            zeros = jnp.zeros((n, CB), F32)
            gain_sum, shift_sum = lax.fori_loop(0, side, body, (zeros, zeros))
            inner = aligned(lax.rem(b, blocks // 2), CB)
            ex6[h, links.me, 0:1, inner] = down(gain_sum)
            ex6[h, links.me, 1:2, inner] = down(shift_sum)
            span = rows + line
            left = jnp.concatenate([hbuf[0:span, :], hbuf[line : line + span, :]], axis=1)
            right = jnp.concatenate([dbuf[0:span, :], dbuf[line : line + span, :]], axis=1)
            full = lax.dot_general(
                left, right, (((0,), (0,)), ((), ())), preferred_element_type=F32
            )
            for dy in range(3):
                left_at, right_at = ((0, 1), (0, 0), (1, 0))[dy]
                for dx in range(3):
                    lane_at = (3 * right_at + 2 - dx) * CB
                    part = full[left_at * CB : (left_at + 1) * CB, lane_at : lane_at + CB]
                    part = jnp.where(keep, part, 0.0)
                    picked = functools.reduce(
                        lambda a, b: a + b,
                        [part[k * group : (k + 1) * group] for k in range(CB // group)],
                    )
                    gwg_ref[pl.ds((dy * 3 + dx) * group, group), lanes] = picked

        links.send(ex6.at[h], ex6_sem.at[0, h], ex6_sem.at[1, h])

    for h in range(2):
        cols = pl.ds(h * half, half)
        links.wait(ex6.at[h], ex6_sem.at[0, h], ex6_sem.at[1, h])
        sums = jnp.sum(ex6[h], axis=0)
        sums1_ref[0:2, cols] = sums
        coef[0:1, cols] = sums[0:1] / total[:, 0:half]
        coef[1:2, cols] = sums[1:2] / total[:, 0:half]
        coef[2:3, cols] = p1_ref[3:4, cols] * p1_ref[1:2, cols]

        @pl.loop(0, side)
        def _(r):
            at = aligned(r, line)
            for q in range(half // CB):
                lanes = pl.ds(h * half + q * CB, CB)
                normed = (red[at, lanes] - p1_ref[0:1, lanes]) * p1_ref[1:2, lanes]
                off = coef[1:2, lanes] + normed * coef[0:1, lanes]
                grad = coef[2:3, lanes] * (mixed[at, lanes] - spread_rows(off, row))
                h2g[at, lanes] = grad.astype(BF)

    for k in range(3):
        loads[k].wait()
    part_cols = 512
    for part in range(C // part_cols):
        cols = pl.ds(part * part_cols, part_cols)
        rwg[cols, :] = lax.dot_general(
            xv[:, cols], h2g[...], (((0,), (0,)), ((), ())), preferred_element_type=F32
        ).astype(BF)
    rwg_store = pltpu.make_async_copy(rwg, rwg_hbm, store_sem.at[0])
    rwg_store.start()
    for part in range(C // part_cols):
        cols = pl.ds(part * part_cols, part_cols)
        for t in range(2):
            at = pl.ds(t * tile, tile)
            out = lax.dot_general(
                h2g[at, :], wr[cols, :], (((1,), (1,)), ((), ())), preferred_element_type=F32
            )
            xv[at, cols] = (out + pre[at, cols]).astype(BF)
    ig_store = pltpu.make_async_copy(xv, ig_hbm, store_sem.at[1])
    ig_store.start()
    rwg_store.wait()
    ig_store.wait()


def pixels_first(field):
    n, side, _, channels = field.shape
    return jnp.transpose(field, (1, 2, 0, 3)).reshape(side * side * n, channels)


def images_first(field, n, side):
    return jnp.transpose(field.reshape(side, side, n, field.shape[1]), (2, 0, 1, 3))


def per_device(
    grp,
    dp,
    image_in,
    slot_mask,
    conv_reduce,
    gain_reduce,
    bias_reduce,
    conv_group,
    gain_group,
    bias_group,
    conv_expand,
    gain_expand,
    bias_expand,
    out_grad,
):
    n, side, _, C = image_in.shape
    W = conv_reduce.shape[1]
    cg = conv_group.shape[3]
    rows = side * side * n
    dims = (n, side, C, W, grp, dp, cg)
    devices = grp * dp
    half = W // 2
    taps_rows = 9 * conv_group.shape[2]
    par1 = jnp.stack([gain_reduce, bias_reduce]).astype(F32)
    par3 = jnp.stack([gain_expand, bias_expand]).astype(F32)
    packed = jnp.concatenate(
        [
            conv_group.reshape(taps_rows, cg),
            gain_group.reshape(1, cg),
            bias_group.reshape(1, cg),
            jnp.zeros((14, cg), BF),
        ]
    )
    x = pixels_first(image_in)
    upstream = pixels_first(out_grad)
    any_spec = pl.BlockSpec(memory_space=pl.ANY)
    vmem = pl.BlockSpec(memory_space=pltpu.VMEM)
    smem = pl.BlockSpec(memory_space=pltpu.SMEM)
    sds = jax.ShapeDtypeStruct
    dma = pltpu.SemaphoreType.DMA
    blocks = W // CB
    span = rows + 2 * side * n
    parts = C // 512

    def params(which):
        return pltpu.CompilerParams(
            collective_id=which, has_side_effects=True, vmem_limit_bytes=VMEM_LIMIT
        )

    red, mixed, p1, p2, wgall = pl.pallas_call(
        functools.partial(ka_kernel, dims),
        name="forward_a",
        out_shape=(
            sds((rows, W), F32),
            sds((rows, W), F32),
            sds((8, W), F32),
            sds((8, W), F32),
            sds((grp, taps_rows + 16, cg), BF),
        ),
        in_specs=[any_spec, any_spec, any_spec, vmem, smem],
        out_specs=(any_spec, any_spec, vmem, vmem, any_spec),
        scratch_shapes=[
            pltpu.VMEM((rows, C), BF),
            pltpu.VMEM((C, W), BF),
            pltpu.VMEM((rows, W), F32),
            pltpu.VMEM((rows, W), F32),
            pltpu.VMEM((grp, taps_rows + 16, cg), BF),
            pltpu.VMEM((blocks, 6 * CB, 2 * CB), BF),
            pltpu.VMEM((span, 3 * CB), BF),
            pltpu.VMEM((devices, 1, 128), F32),
            pltpu.VMEM((2, devices, 2, half), F32),
            pltpu.VMEM((2, devices, 2, half), F32),
            dma((5,)),
            dma((4,)),
            dma((2, grp - 1)),
            dma((2,)),
            dma((2, 2)),
            dma((2, 2)),
        ],
        compiler_params=params(0),
    )(x, conv_reduce, packed, par1, slot_mask)

    block_out, pre, h2g, ewg, sums3, sums2 = pl.pallas_call(
        functools.partial(kb_kernel, dims),
        name="middle_b",
        out_shape=(
            sds((rows, C), BF),
            sds((rows, C), F32),
            sds((rows, W), BF),
            sds((W, C), BF),
            sds((2, C), F32),
            sds((2, W), F32),
        ),
        in_specs=[any_spec, vmem, any_spec, any_spec, any_spec, vmem, smem],
        out_specs=(any_spec, any_spec, any_spec, any_spec, vmem, vmem),
        scratch_shapes=[
            pltpu.VMEM((rows, W), F32),
            pltpu.VMEM((W, C), BF),
            pltpu.VMEM((rows, W), BF),
            pltpu.VMEM((rows, C), F32),
            pltpu.VMEM((rows, C), BF),
            pltpu.VMEM((rows, C), BF),
            pltpu.VMEM((rows, C), BF),
            pltpu.VMEM((rows, W), BF),
            pltpu.VMEM((8, C), F32),
            pltpu.VMEM((devices, 1, 128), F32),
            pltpu.VMEM((parts, devices, 2, 512), F32),
            pltpu.VMEM((parts, devices, 2, 512), F32),
            dma((10,)),
            dma((4,)),
            dma((2,)),
            dma((2, parts)),
            dma((2, parts)),
            dma((2, 2)),
        ],
        compiler_params=params(1),
    )(mixed, p2, conv_expand, x, upstream, par3, slot_mask)

    image_grad, rwg, gwg, sums1 = pl.pallas_call(
        functools.partial(kc_kernel, dims),
        name="backward_c",
        out_shape=(
            sds((rows, C), BF),
            sds((C, W), BF),
            sds((taps_rows, W), F32),
            sds((2, W), F32),
        ),
        in_specs=[any_spec] * 3 + [vmem] * 4 + [any_spec] * 3 + [smem],
        out_specs=(any_spec, any_spec, vmem, vmem),
        scratch_shapes=[
            pltpu.VMEM((rows, W), BF),
            pltpu.VMEM((rows, W), F32),
            pltpu.VMEM((rows, W), F32),
            pltpu.VMEM((rows, C), BF),
            pltpu.VMEM((C, W), BF),
            pltpu.VMEM((rows, C), F32),
            pltpu.VMEM((C, W), BF),
            pltpu.VMEM((blocks, 2 * CB, 6 * CB), BF),
            pltpu.VMEM((span, 3 * CB), BF),
            pltpu.VMEM((span, CB), BF),
            pltpu.VMEM((8, W), F32),
            pltpu.VMEM((2, devices, 2, half), F32),
            dma((3, blocks)),
            dma((3,)),
            dma((2,)),
            dma((2, 2)),
        ],
        compiler_params=params(2),
    )(h2g, mixed, red, p1, p2, sums2, wgall, x, conv_reduce, pre, slot_mask)

    ewg_sum, rwg_sum, gwg_sum = lax.psum((ewg, rwg, gwg.astype(BF)), ("grp", "dp"))
    group_wgrad = lax.dynamic_slice_in_dim(gwg_sum, lax.axis_index("grp") * cg, cg, 1)
    group_wgrad = group_wgrad.astype(F32).reshape(3, 3, conv_group.shape[2], cg)
    own = lax.dynamic_slice_in_dim(sums2, lax.axis_index("grp") * cg, cg, 1)
    return (
        images_first(block_out, n, side),
        images_first(image_grad, n, side),
        rwg_sum.astype(F32),
        sums1[0],
        sums1[1],
        group_wgrad,
        own[0],
        own[1],
        ewg_sum.astype(F32),
        sums3[0],
        sums3[1],
    )


def solution(mesh):
    placed = (
        P(("grp", "dp"), None, None, None),
        P(("grp", "dp")),
        P(),
        P(),
        P(),
        P(None, None, None, "grp"),
        P("grp"),
        P("grp"),
        P(),
        P(),
        P(),
        P(("grp", "dp"), None, None, None),
    )
    return jax.shard_map(
        functools.partial(per_device, mesh.shape["grp"], mesh.shape["dp"]),
        mesh=mesh,
        in_specs=placed,
        out_specs=(
            P(("grp", "dp"), None, None, None),
            P(("grp", "dp"), None, None, None),
            P(),
            P(),
            P(),
            P(None, None, None, "grp"),
            P("grp"),
            P("grp"),
            P(),
            P(),
            P(),
        ),
        check_vma=False,
    )
```

```python
import functools

import jax
import jax.numpy as jnp
from jax import lax
from jax.experimental import pallas as pl
from jax.experimental.pallas import tpu as pltpu
from jax.sharding import PartitionSpec as P

EPS = 1e-05
BF = jnp.bfloat16
F32 = jnp.float32
MESH = pl.DeviceIdType.MESH
CB = 128
VMEM_LIMIT = 61952 * 1024


def aligned(index, size):
    return pl.ds(pl.multiple_of(index * size, size), size)


def sigmoid(values):
    return 0.5 * jnp.tanh(0.5 * values) + 0.5


def fold(values, images):
    rows, cols = values.shape
    return jnp.sum(values.reshape(rows // images, images, cols), axis=0)


def down(values):
    return jnp.sum(values, axis=0, keepdims=True)


def spread_rows(values, row):
    rows, cols = values.shape
    images = row.shape[0]
    return (values.reshape(rows // images, images, cols) * wide(row, cols)[None]).reshape(rows, cols)


class Links:
    def __init__(self, grp, dp):
        self.grp, self.dp = grp, dp
        self.count = grp * dp
        self.g, self.d = lax.axis_index("grp"), lax.axis_index("dp")
        self.me = self.g * dp + self.d

    def peer(self, step):
        target = lax.rem(self.me + step, self.count)
        return (target // self.dp, lax.rem(target, self.dp))

    def greet(self):
        barrier = pltpu.get_barrier_semaphore()

        @pl.loop(1, self.count)
        def _(step):
            pl.semaphore_signal(barrier, inc=1, device_id=self.peer(step), device_id_type=MESH)

    def greeted(self):
        pl.semaphore_wait(pltpu.get_barrier_semaphore(), self.count - 1)

    def send(self, buf, send_sem, recv_sem):
        @pl.loop(1, self.count)
        def _(step):
            pltpu.make_async_remote_copy(
                src_ref=buf.at[self.me],
                dst_ref=buf.at[self.me],
                send_sem=send_sem,
                recv_sem=recv_sem,
                device_id=self.peer(step),
                device_id_type=MESH,
            ).start()

    def wait(self, buf, send_sem, recv_sem):
        others = buf.at[pl.ds(0, self.count - 1)]
        copy = pltpu.make_async_remote_copy(
            src_ref=others,
            dst_ref=others,
            send_sem=send_sem,
            recv_sem=recv_sem,
            device_id=self.peer(1),
            device_id_type=MESH,
        )
        copy.wait_recv()
        copy.wait_send()


def index_bits(grp, dp):
    ones = lambda count: [1 << k for k in range(count.bit_length() - 1)]
    g_bits = [("grp", w) for w in ones(grp)]
    d_bits = [("dp", w) for w in ones(dp)]
    low = len(d_bits) // 2
    return g_bits[:1], g_bits[1:], d_bits[:low], d_bits[low:]


class Reduction:
    def __init__(self, links, buf, recv, out, sems, own_sems):
        self.links, self.buf, self.recv, self.out = links, buf, recv, out
        self.sems, self.own_sems = sems, own_sems
        core, y, x, z = index_bits(links.grp, links.dp)
        orders = (core + x + y + z, core + y + x + z, core + z + x + y)
        unit = 16 * links.count
        units = buf.shape[0] // unit
        last = units // 4
        sizes = ((units - last + 1) // 2, (units - last) // 2, last)
        self.parts = []
        start = 0
        for order, size in zip(orders, sizes):
            if size:
                self.parts.append(dict(start=start, size=size * unit, lo=start, order=order))
            start += size * unit
        self.bits = len(orders[0])
        self.stage = 0

    def place(self, bit):
        axis, weight = bit
        at = self.links.g if axis == "grp" else self.links.d
        value = lax.rem(at // weight, 2)
        other = at + weight * (1 - 2 * value)
        return value, (other, self.links.d) if axis == "grp" else (self.links.g, other)

    def copy(self, index, part):
        rows = lambda lo, size: pl.ds(pl.multiple_of(lo, 16), size)
        halving = self.stage < self.bits
        bit = part["order"][self.stage if halving else 2 * self.bits - 1 - self.stage]
        value, device = self.place(bit)
        if halving:
            half = part["size"] // 2
            src = self.buf.at[rows(part["lo"] + (1 - value) * half, half)]
            dst = self.recv.at[rows(part["start"], half)]
        else:
            here = self.buf if self.stage == self.bits else self.out
            src = here.at[rows(part["lo"], part["size"])]
            dst = self.out.at[rows(part["lo"], part["size"])]
        return value, pltpu.make_async_remote_copy(
            src_ref=src,
            dst_ref=dst,
            send_sem=self.sems.at[0, index, self.stage],
            recv_sem=self.sems.at[1, index, self.stage],
            device_id=device,
            device_id_type=MESH,
        )

    def start(self):
        for index, part in enumerate(self.parts):
            self.copy(index, part)[1].start()

    def advance(self):
        for index, part in enumerate(self.parts):
            value, copy = self.copy(index, part)
            copy.wait()
            if self.stage < self.bits:
                half = part["size"] // 2
                keep, base = part["lo"] + value * half, part["start"]
                chunk = max(c for c in range(16, 513, 16) if half % c == 0)

                @pl.loop(0, half // chunk)
                def _(k):
                    at = pl.ds(pl.multiple_of(keep + k * chunk, 16), chunk)
                    more = self.recv[pl.ds(pl.multiple_of(base + k * chunk, 16), chunk), :]
                    self.buf[at, :] = (self.buf[at, :].astype(F32) + more.astype(F32)).astype(BF)

                part.update(lo=keep, size=half, start=base + half)
                if self.stage == self.bits - 1:
                    at = pl.ds(pl.multiple_of(keep, 16), half)
                    part["own"] = pltpu.make_async_copy(
                        self.buf.at[at], self.out.at[at], self.own_sems.at[index]
                    )
                    part["own"].start()
            else:
                if self.stage == self.bits:
                    part["own"].wait()
                part.update(lo=part["lo"] - value * part["size"], size=2 * part["size"])
        self.stage += 1
        if self.stage < 2 * self.bits:
            self.start()

    def finish(self, upto=None):
        while self.stage < 2 * self.bits:
            self.advance()


def wide(row, cols):
    return jnp.concatenate([row] * (cols // 128), axis=-1)


def row_weights(mask_ref, images):
    at = lax.broadcasted_iota(jnp.int32, (images, 128), 0)
    column = jnp.zeros((images, 128), F32)
    count = jnp.float32(0.0)
    for i in range(images):
        value = mask_ref[i].astype(F32)
        column = jnp.where(at == i, value, column)
        count = count + value
    return column, count


def merge_stats(buf, counts, cols):
    each = wide(counts, cols)
    total = jnp.sum(each, axis=0)
    parts = buf[...]
    means, squares = parts[:, 0:1], parts[:, 1:2]
    average = jnp.sum(each * means, axis=0) / total
    gap = means - average
    spread = jnp.sum(squares + each * gap * gap, axis=0) / total
    return average, lax.rsqrt(spread + EPS)


def dense_taps(shard):
    group = 32
    row = lax.broadcasted_iota(jnp.int32, (CB, CB), 0) // group
    col = lax.broadcasted_iota(jnp.int32, (CB, CB), 1) // group
    keep = row == col
    zero = jnp.zeros((CB, CB), BF)

    def block(row_tap, col_tap):
        start = (row_tap * 3 + col_tap) * group
        tile = shard(start, group).astype(F32)
        full = jnp.concatenate([tile] * (CB // group), axis=0)
        return jnp.where(keep, full, 0.0).astype(BF)

    return block, zero


def shifted(values, images):
    edge = jnp.zeros((images, values.shape[1]), F32)
    return (
        jnp.concatenate([edge, values[:-images]], axis=0),
        jnp.concatenate([values[images:], edge], axis=0),
    )


def local_stats(field, cols, mean_of, rows, chunk, images, row, inverse, width):
    mean = down(mean_of * wide(row, width)) * wide(inverse, width)

    def body(k, acc):
        gap = field[aligned(k, chunk), cols] - mean
        return acc + fold(gap * gap, images)

    squares = lax.fori_loop(0, rows // chunk, body, jnp.zeros((images, width), F32))
    return mean, down(squares * wide(row, width))


def ka_kernel(
    dims,
    x_hbm,
    wr_hbm,
    wg_hbm,
    par_ref,
    mask_ref,
    red_hbm,
    mixed_hbm,
    p1_ref,
    p2_ref,
    wgall_hbm,
    xv,
    wr,
    red,
    mixed,
    wgall,
    taps,
    hbuf,
    cnt,
    ex1,
    ex2,
    load_sem,
    store_sem,
    gather_sem,
    cnt_sem,
    ex1_sem,
    ex2_sem,
):
    n, side, C, W, grp, dp, cg = dims
    rows = side * side * n
    line = side * n
    half = W // 2
    tile = rows // 2
    links = Links(grp, dp)
    links.greet()
    w_loads = [
        pltpu.make_async_copy(
            wr_hbm.at[:, pl.ds(h * half, half)], wr.at[:, pl.ds(h * half, half)], load_sem.at[h]
        )
        for h in range(2)
    ]
    x_loads = [
        pltpu.make_async_copy(
            x_hbm.at[pl.ds(h * tile, tile), :], xv.at[pl.ds(h * tile, tile), :], load_sem.at[2 + h]
        )
        for h in range(2)
    ]
    w_loads[0].start()
    x_loads[0].start()
    x_loads[1].start()
    w_loads[1].start()
    own = pltpu.make_async_copy(wg_hbm, wgall.at[links.g], load_sem.at[4])
    own.start()

    row, valid = row_weights(mask_ref, n)
    local = jnp.full((1, 128), 1.0, F32) * (valid * float(side * side))
    cnt[links.me] = local
    inverse = 1.0 / jnp.maximum(local, 1.0)
    hbuf[...] = jnp.zeros(hbuf.shape, BF)
    links.greeted()
    links.send(cnt, cnt_sem.at[0], cnt_sem.at[1])
    gathers = []
    for k in range(1, grp):
        copy = pltpu.make_async_remote_copy(
            src_ref=wg_hbm,
            dst_ref=wgall.at[links.g],
            send_sem=gather_sem.at[0, k - 1],
            recv_sem=gather_sem.at[1, k - 1],
            device_id=(lax.rem(links.g + k, grp), links.d),
            device_id_type=MESH,
        )
        copy.start()
        gathers.append(copy)

    for h in range(2):
        w_loads[h].wait()
        cols = pl.ds(h * half, half)
        total = jnp.zeros((n, half), F32)
        for t in range(2):
            if h == 0:
                x_loads[t].wait()
            at = pl.ds(t * tile, tile)
            out = jnp.dot(xv[at, :], wr[:, cols], preferred_element_type=F32)
            red[at, cols] = out
            total += fold(out, n)
        mean, squares = local_stats(red, cols, total, rows, line, n, row, inverse, half)
        ex1[h, links.me, 0:1, :] = mean
        ex1[h, links.me, 1:2, :] = squares
        if h == 0:
            links.wait(cnt, cnt_sem.at[0], cnt_sem.at[1])
        links.send(ex1.at[h], ex1_sem.at[0, h], ex1_sem.at[1, h])
    red_store = pltpu.make_async_copy(red, red_hbm, store_sem.at[0])
    red_store.start()

    own.wait()
    for copy in gathers:
        copy.wait()
    store_wg = pltpu.make_async_copy(wgall, wgall_hbm, store_sem.at[1])
    store_wg.start()
    blocks = W // CB
    per_shard = cg // CB

    @pl.loop(0, blocks)
    def _(b):
        shard_at, lane = b // per_shard, aligned(lax.rem(b, per_shard), CB)
        block, zero = dense_taps(lambda start, size: wgall[shard_at, pl.ds(start, size), lane])
        for dx in range(3):
            taps[b, pl.ds(dx * CB, CB), 0:CB] = block(0, dx)
            taps[b, pl.ds(dx * CB, CB), CB : 2 * CB] = zero
            taps[b, pl.ds((3 + dx) * CB, CB), 0:CB] = block(1, dx)
            taps[b, pl.ds((3 + dx) * CB, CB), CB : 2 * CB] = block(2, dx)

    for h in range(2):
        links.wait(ex1.at[h], ex1_sem.at[0, h], ex1_sem.at[1, h])
        cols = pl.ds(h * half, half)
        average, scale = merge_stats(ex1.at[h], cnt[...], half)
        p1_ref[0:1, cols] = average
        p1_ref[1:2, cols] = scale

        @pl.loop(h * blocks // 2, (h + 1) * blocks // 2)
        def _(b):
            lanes = aligned(b, CB)
            mean, rstd = p1_ref[0:1, lanes], p1_ref[1:2, lanes]
            gain, shift = par_ref[0:1, lanes], par_ref[1:2, lanes]

            @pl.loop(0, side)
            def _(r):
                act = (red[aligned(r, line), lanes] - mean) * rstd * gain + shift
                hidden = act * sigmoid(act)
                left, right = shifted(hidden, n)
                to = aligned(r + 1, line)
                hbuf[to, 0:CB] = left.astype(BF)
                hbuf[to, CB : 2 * CB] = hidden.astype(BF)
                hbuf[to, 2 * CB : 3 * CB] = right.astype(BF)

            lhs = jnp.concatenate([hbuf[0 : rows + line, :], hbuf[line : rows + 2 * line, :]], axis=1)
            out = jnp.dot(lhs, taps[b], preferred_element_type=F32)
            field = out[0:rows, 0:CB] + out[line : line + rows, CB:]
            mixed[:, lanes] = field
            mean, squares = local_stats(
                mixed, lanes, fold(field, n), rows, line, n, row, inverse, CB
            )
            inner = aligned(lax.rem(b, blocks // 2), CB)
            ex2[h, links.me, 0:1, inner] = mean
            ex2[h, links.me, 1:2, inner] = squares

        links.send(ex2.at[h], ex2_sem.at[0, h], ex2_sem.at[1, h])
        pltpu.make_async_copy(mixed.at[:, cols], mixed_hbm.at[:, cols], store_sem.at[2 + h]).start()

    count = jnp.sum(wide(cnt[...], W), axis=0)
    p1_ref[2:3, :] = count
    p2_ref[2:3, :] = count
    extra = jnp.concatenate(
        [wgall[k, pl.ds(9 * 32, 16), :].astype(F32) for k in range(grp)], axis=1
    )
    p2_ref[3:5, :] = extra[0:2]
    p1_ref[3:5, :] = par_ref[0:2, :]
    for h in range(2):
        links.wait(ex2.at[h], ex2_sem.at[0, h], ex2_sem.at[1, h])
        cols = pl.ds(h * half, half)
        average, scale = merge_stats(ex2.at[h], cnt[...], half)
        p2_ref[0:1, cols] = average
        p2_ref[1:2, cols] = scale
    red_store.wait()
    store_wg.wait()
    for h in range(2):
        cols = pl.ds(h * half, half)
        pltpu.make_async_copy(mixed.at[:, cols], mixed_hbm.at[:, cols], store_sem.at[2 + h]).wait()


def kb_kernel(
    dims,
    mixed_hbm,
    p2_ref,
    we_hbm,
    x_hbm,
    dout_hbm,
    par_ref,
    mask_ref,
    out_hbm,
    pre_hbm,
    h2g_hbm,
    ewg_hbm,
    sums3_ref,
    sums2_ref,
    mixed,
    we,
    h2,
    expd,
    xe,
    dout,
    n3,
    h2g,
    stat3,
    cnt,
    ex3,
    ex4,
    load_sem,
    store_sem,
    cnt_sem,
    ex3_sem,
    ex4_sem,
    ex5_sem,
):
    n, side, C, W, grp, dp, cg = dims
    rows = side * side * n
    line = side * n
    half = W // 2
    tile = rows // 2
    links = Links(grp, dp)
    links.greet()
    part_cols = 512
    parts = C // part_cols
    pieces = 7
    piece = rows // pieces
    m_loads = [
        pltpu.make_async_copy(
            mixed_hbm.at[pl.ds(k * piece, piece), :],
            mixed.at[pl.ds(k * piece, piece), :],
            load_sem.at[k],
        )
        for k in range(pieces)
    ]
    for copy in m_loads:
        copy.start()
    we_load = pltpu.make_async_copy(we_hbm, we, load_sem.at[pieces])
    we_load.start()
    x_load = pltpu.make_async_copy(x_hbm, xe, load_sem.at[pieces + 1])
    x_load.start()
    d_load = pltpu.make_async_copy(dout_hbm, dout, load_sem.at[pieces + 2])
    d_load.start()
    row, valid = row_weights(mask_ref, n)
    local = jnp.full((1, 128), 1.0, F32) * (valid * float(side * side))
    cnt[links.me] = local
    inverse = 1.0 / jnp.maximum(local, 1.0)
    links.greeted()
    links.send(cnt, cnt_sem.at[0], cnt_sem.at[1])

    step = 256
    lines = rows // line
    for k in range(pieces):
        m_loads[k].wait()

        @pl.loop(k * lines // pieces, (k + 1) * lines // pieces)
        def _(r):
            at = aligned(r, line)
            for q in range(W // step):
                lanes = pl.ds(q * step, step)
                normed = (mixed[at, lanes] - p2_ref[0:1, lanes]) * p2_ref[1:2, lanes]
                act = normed * p2_ref[3:4, lanes] + p2_ref[4:5, lanes]
                h2[at, lanes] = (act * sigmoid(act)).astype(BF)

    we_load.wait()
    links.wait(cnt, cnt_sem.at[0], cnt_sem.at[1])
    for part in range(parts):
        cols = pl.ds(part * part_cols, part_cols)
        total = jnp.zeros((n, part_cols), F32)
        for t in range(2):
            at = pl.ds(t * tile, tile)
            out = jnp.dot(h2[at, :], we[:, cols], preferred_element_type=F32)
            expd[at, cols] = out
            total += fold(out, n)
        mean, squares = local_stats(expd, cols, total, rows, line, n, row, inverse, part_cols)
        ex3[part, links.me, 0:1, :] = mean
        ex3[part, links.me, 1:2, :] = squares
        links.send(ex3.at[part], ex3_sem.at[0, part], ex3_sem.at[1, part])

    x_load.wait()
    d_load.wait()
    step = 128
    for part in range(parts):
        cols = pl.ds(part * part_cols, part_cols)
        links.wait(ex3.at[part], ex3_sem.at[0, part], ex3_sem.at[1, part])
        average, scale = merge_stats(ex3.at[part], cnt[...], part_cols)
        stat3[0:1, cols] = average
        stat3[1:2, cols] = scale

        @pl.loop(0, part_cols // step)
        def _(q):
            lanes = pl.ds(pl.multiple_of(part * part_cols + q * step, step), step)
            mean, rstd = stat3[0:1, lanes], stat3[1:2, lanes]
            gain, shift = par_ref[0:1, lanes], par_ref[1:2, lanes]

            def body(r, sums):
                at = aligned(r, line)
                normed = (expd[at, lanes] - mean) * rstd
                summed = normed * gain + shift + xe[at, lanes].astype(F32)
                sig = sigmoid(summed)
                silu = summed * sig
                grad = spread_rows(dout[at, lanes].astype(F32), row) * (sig + silu * (1.0 - sig))
                dout[at, lanes] = spread_rows(silu, row).astype(BF)
                expd[at, lanes] = grad
                n3[at, lanes] = normed.astype(BF)
                return sums[0] + fold(grad * normed, n), sums[1] + fold(grad, n)

            zeros = jnp.zeros((n, step), F32)
            gain_sum, shift_sum = lax.fori_loop(0, lines, body, (zeros, zeros))
            inner = aligned(q, step)
            ex4[part, links.me, 0:1, inner] = down(gain_sum)
            ex4[part, links.me, 1:2, inner] = down(shift_sum)

        links.send(ex4.at[part], ex4_sem.at[0, part], ex4_sem.at[1, part])
    out_store = pltpu.make_async_copy(dout, out_hbm, store_sem.at[0])
    out_store.start()
    pre_store = pltpu.make_async_copy(expd, pre_hbm, store_sem.at[1])
    pre_store.start()

    total = jnp.sum(wide(cnt[...], part_cols), axis=0)
    for part in range(parts):
        cols = pl.ds(part * part_cols, part_cols)
        links.wait(ex4.at[part], ex4_sem.at[0, part], ex4_sem.at[1, part])
        sums = jnp.sum(ex4[part], axis=0)
        sums3_ref[0:2, cols] = sums
        stat3[2:3, cols] = sums[0:1] / total
        stat3[3:4, cols] = sums[1:2] / total
        stat3[4:5, cols] = par_ref[0:1, cols] * stat3[1:2, cols]

        @pl.loop(0, lines)
        def _(r):
            at = aligned(r, line)
            for q in range(part_cols // step):
                lanes = pl.ds(part * part_cols + q * step, step)
                off = stat3[3:4, lanes] + n3[at, lanes].astype(F32) * stat3[2:3, lanes]
                value = stat3[4:5, lanes] * (expd[at, lanes] - spread_rows(off, row))
                xe[at, lanes] = value.astype(BF)

    ex5 = ex3
    for h in range(2):
        cols = pl.ds(h * half, half)
        for t in range(2):
            at = pl.ds(t * tile, tile)
            h2g[at, cols] = lax.dot_general(
                xe[at, :], we[cols, :], (((1,), (1,)), ((), ())), preferred_element_type=F32
            ).astype(BF)

        @pl.loop(0, half // step)
        def _(q):
            lanes = pl.ds(pl.multiple_of(h * half + q * step, step), step)
            mean, rstd = p2_ref[0:1, lanes], p2_ref[1:2, lanes]
            gain, shift = p2_ref[3:4, lanes], p2_ref[4:5, lanes]

            def body(r, sums):
                at = aligned(r, line)
                normed = (mixed[at, lanes] - mean) * rstd
                act = normed * gain + shift
                sig = sigmoid(act)
                grad = h2g[at, lanes].astype(F32) * (sig + act * sig * (1.0 - sig))
                return sums[0] + fold(grad * normed, n), sums[1] + fold(grad, n)

            zeros = jnp.zeros((n, step), F32)
            gain_sum, shift_sum = lax.fori_loop(0, lines, body, (zeros, zeros))
            inner = aligned(q, step)
            ex5[h, links.me, 0:1, inner] = down(gain_sum)
            ex5[h, links.me, 1:2, inner] = down(shift_sum)

        links.send(ex5.at[h], ex5_sem.at[0, h], ex5_sem.at[1, h])
    h2g_store = pltpu.make_async_copy(h2g, h2g_hbm, store_sem.at[2])
    h2g_store.start()

    ewg = we
    for part in range(parts):
        cols = pl.ds(part * part_cols, part_cols)
        ewg[:, cols] = lax.dot_general(
            h2[...], xe[:, cols], (((0,), (0,)), ((), ())), preferred_element_type=F32
        ).astype(BF)
    ewg_store = pltpu.make_async_copy(ewg, ewg_hbm, store_sem.at[3])
    ewg_store.start()
    for h in range(2):
        links.wait(ex5.at[h], ex5_sem.at[0, h], ex5_sem.at[1, h])
        sums2_ref[0:2, pl.ds(h * half, half)] = jnp.sum(ex5[h], axis=0)
    out_store.wait()
    pre_store.wait()
    h2g_store.wait()
    ewg_store.wait()


def kc_kernel(
    dims,
    h2g_hbm,
    mixed_hbm,
    red_hbm,
    p1_ref,
    p2_ref,
    sums2_ref,
    wgall_ref,
    x_hbm,
    wr_hbm,
    pre_hbm,
    ewg_hbm,
    mask_ref,
    ig_hbm,
    rwg_hbm,
    ewg_out_hbm,
    gwg_hbm,
    sums1_ref,
    h2g,
    mixed,
    red,
    xv,
    wr,
    pre,
    ewg,
    ewg_in,
    rwg,
    rwg_in,
    gwg,
    gwg_in,
    taps,
    dbuf,
    hbuf,
    coef,
    ex6,
    block_sem,
    load_sem,
    store_sem,
    ex6_sem,
    ewg_sem,
    rwg_sem,
    gwg_sem,
    own_sem,
):
    n, side, C, W, grp, dp, cg = dims
    rows = side * side * n
    line = side * n
    half = W // 2
    tile = rows // 2
    blocks = W // CB
    per_shard = cg // CB
    links = Links(grp, dp)
    links.greet()

    def block_loads(b):
        lanes = aligned(b, CB)
        return [
            pltpu.make_async_copy(src.at[:, lanes], dst.at[:, lanes], block_sem.at[k, b])
            for k, (src, dst) in enumerate(((h2g_hbm, h2g), (mixed_hbm, mixed), (red_hbm, red)))
        ]

    @pl.loop(0, blocks)
    def _(b):
        for copy in block_loads(b):
            copy.start()

    ewg_loads = [
        pltpu.make_async_copy(
            ewg_hbm.at[:, pl.ds(k * 128, 128)], ewg.at[pl.ds(k * W, W), :], load_sem.at[4 + k]
        )
        for k in range(C // 128)
    ]
    for copy in ewg_loads:
        copy.start()
    loads = [
        pltpu.make_async_copy(src, dst, load_sem.at[k])
        for k, (src, dst) in enumerate(((x_hbm, xv), (wr_hbm, wr)))
    ]
    for copy in loads:
        copy.start()
    part_cols = 512
    pre_loads = [
        pltpu.make_async_copy(
            pre_hbm.at[pl.ds(t * tile, tile), pl.ds(part * part_cols, part_cols)],
            pre.at[t],
            load_sem.at[2 + t],
        )
        for part in range(C // part_cols)
        for t in range(2)
    ]
    pre_loads[0].start()
    pre_loads[1].start()
    gwg[...] = jnp.zeros(gwg.shape, BF)
    half_rows = half // 128 * C
    sums = [
        Reduction(
            links,
            *(ref.at[pl.ds(h * half_rows, half_rows)] for ref in (rwg, rwg_in, rwg_hbm)),
            rwg_sem.at[h],
            own_sem.at[h],
        )
        for h in range(2)
    ]
    ewg_sum = Reduction(links, ewg, ewg_in, ewg_out_hbm, ewg_sem, own_sem.at[2])
    gwg_sum = Reduction(links, gwg, gwg_in, gwg_hbm, gwg_sem, own_sem.at[3])
    row, valid = row_weights(mask_ref, n)
    dbuf[...] = jnp.zeros(dbuf.shape, BF)
    hbuf[...] = jnp.zeros(hbuf.shape, BF)
    total = p2_ref[2:3, :]
    coef[0:1, :] = sums2_ref[0:1, :] / total
    coef[1:2, :] = sums2_ref[1:2, :] / total
    coef[2:3, :] = p2_ref[3:4, :] * p2_ref[1:2, :]

    @pl.loop(0, blocks)
    def _(b):
        shard_at, lane = b // per_shard, aligned(lax.rem(b, per_shard), CB)
        block, zero = dense_taps(lambda start, size: wgall_ref[shard_at, pl.ds(start, size), lane])
        for dx in range(3):
            taps[b, 0:CB, pl.ds(dx * CB, CB)] = block(2, 2 - dx)
            taps[b, CB : 2 * CB, pl.ds(dx * CB, CB)] = zero
            taps[b, 0:CB, pl.ds((3 + dx) * CB, CB)] = block(1, 2 - dx)
            taps[b, CB : 2 * CB, pl.ds((3 + dx) * CB, CB)] = block(0, 2 - dx)

    links.greeted()
    for copy in ewg_loads:
        copy.wait()
    ewg_sum.start()
    group = 32
    keep = (
        lax.broadcasted_iota(jnp.int32, (CB, CB), 0) // group
        == lax.broadcasted_iota(jnp.int32, (CB, CB), 1) // group
    )
    def conv_block(h, b):
        for copy in block_loads(b):
            copy.wait()
        lanes = pl.ds(b * CB, CB)

        @pl.loop(0, side)
        def _(r):
            at = aligned(r, line)
            normed = (mixed[at, lanes] - p2_ref[0:1, lanes]) * p2_ref[1:2, lanes]
            act = normed * p2_ref[3:4, lanes] + p2_ref[4:5, lanes]
            sig = sigmoid(act)
            grad = h2g[at, lanes].astype(F32) * (sig + act * sig * (1.0 - sig))
            off = coef[1:2, lanes] + normed * coef[0:1, lanes]
            grad = coef[2:3, lanes] * (grad - spread_rows(off, row))
            left, right = shifted(grad, n)
            to = aligned(r + 1, line)
            dbuf[to, 0:CB] = left.astype(BF)
            dbuf[to, CB : 2 * CB] = grad.astype(BF)
            dbuf[to, 2 * CB : 3 * CB] = right.astype(BF)

        lhs = jnp.concatenate([dbuf[0 : rows + line, :], dbuf[line : rows + 2 * line, :]], axis=1)
        out = lax.dot_general(
            lhs, taps[b], (((1,), (1,)), ((), ())), preferred_element_type=F32
        )
        mixed[:, lanes] = out[0:rows, 0:CB] + out[line : line + rows, CB:]
        mean, rstd = p1_ref[0:1, lanes], p1_ref[1:2, lanes]
        gain, shift = p1_ref[3:4, lanes], p1_ref[4:5, lanes]

        def body(r, sums):
            at = aligned(r, line)
            normed = (red[at, lanes] - mean) * rstd
            act = normed * gain + shift
            sig = sigmoid(act)
            silu = act * sig
            hbuf[aligned(r + 1, line), :] = silu.astype(BF)
            grad = mixed[at, lanes].astype(BF).astype(F32) * (sig + silu * (1.0 - sig))
            mixed[at, lanes] = grad
            return sums[0] + fold(grad * normed, n), sums[1] + fold(grad, n)

        zeros = jnp.zeros((n, CB), F32)
        gain_sum, shift_sum = lax.fori_loop(0, side, body, (zeros, zeros))
        inner = pl.ds(b % (blocks // 2) * CB, CB)
        ex6[h, links.me, 0:1, inner] = down(gain_sum)
        ex6[h, links.me, 1:2, inner] = down(shift_sum)
        span = rows + line
        left = jnp.concatenate([hbuf[0:span, :], hbuf[line : line + span, :]], axis=1)
        right = jnp.concatenate([dbuf[0:span, :], dbuf[line : line + span, :]], axis=1)
        full = lax.dot_general(
            left, right, (((0,), (0,)), ((), ())), preferred_element_type=F32
        )
        for dy in range(3):
            left_at, right_at = ((0, 1), (0, 0), (1, 0))[dy]
            for dx in range(3):
                lane_at = (3 * right_at + 2 - dx) * CB
                part = full[left_at * CB : (left_at + 1) * CB, lane_at : lane_at + CB]
                part = jnp.where(keep, part, 0.0)
                picked = functools.reduce(
                    lambda a, b: a + b,
                    [part[k * group : (k + 1) * group] for k in range(CB // group)],
                )
                gwg[pl.ds((b * 9 + dy * 3 + dx) * group, group), :] = picked.astype(BF)

    def reduce_half(h):
        cols = pl.ds(h * half, half)
        links.wait(ex6.at[h], ex6_sem.at[0, h], ex6_sem.at[1, h])
        both = jnp.sum(ex6[h], axis=0)
        sums1_ref[0:2, cols] = both
        coef[3:4, cols] = both[0:1] / total[:, 0:half]
        coef[4:5, cols] = both[1:2] / total[:, 0:half]
        coef[5:6, cols] = p1_ref[3:4, cols] * p1_ref[1:2, cols]

        @pl.loop(0, side)
        def _(r):
            at = aligned(r, line)
            for q in range(half // CB):
                lanes = pl.ds(h * half + q * CB, CB)
                normed = (red[at, lanes] - p1_ref[0:1, lanes]) * p1_ref[1:2, lanes]
                off = coef[4:5, lanes] + normed * coef[3:4, lanes]
                grad = coef[5:6, lanes] * (mixed[at, lanes] - spread_rows(off, row))
                h2g[at, lanes] = grad.astype(BF)

        if h == 0:
            loads[0].wait()
        big = C // 2
        for k in range(2):
            out = lax.dot_general(
                xv[:, pl.ds(k * big, big)],
                h2g[:, cols],
                (((0,), (0,)), ((), ())),
                preferred_element_type=F32,
            )
            for q in range(half // 128):
                start = (h * (half // 128) + q) * C + k * big
                rwg[pl.ds(start, big), :] = out[:, q * 128 : (q + 1) * 128].astype(BF)
        sums[h].start()

    for b in range(blocks):
        h = b * 2 // blocks
        conv_block(h, b)
        if b % (blocks // 2) == blocks // 2 - 1:
            links.send(ex6.at[h], ex6_sem.at[0, h], ex6_sem.at[1, h])
        if b in (1, 3, 4, 5, 6):
            ewg_sum.advance()
        if b == blocks - 2:
            reduce_half(0)
    ewg_sum.advance()
    gwg_sum.start()
    reduce_half(1)
    ewg_sum.advance()
    sums[0].advance()
    gwg_sum.advance()

    loads[1].wait()
    ig_stores = []
    for part in range(C // part_cols):
        cols = pl.ds(part * part_cols, part_cols)
        for t in range(2):
            at = pl.ds(t * tile, tile)
            out = lax.dot_general(
                h2g[at, :], wr[cols, :], (((1,), (1,)), ((), ())), preferred_element_type=F32
            )
            pre_loads[2 * part + t].wait()
            xv[at, cols] = (out + pre[t]).astype(BF)
            if 2 * part + t + 2 < len(pre_loads):
                pre_loads[2 * part + t + 2].start()
        store = pltpu.make_async_copy(xv.at[:, cols], ig_hbm.at[:, cols], store_sem.at[part])
        store.start()
        ig_stores.append(store)
        if part < 3:
            ewg_sum.advance()
            sums[1].advance()
            sums[0].advance()
            gwg_sum.advance()
    ewg_sum.finish()
    for stage in range(2 * ewg_sum.bits):
        for each in (sums[0], gwg_sum, sums[1]):
            if each.stage < 2 * each.bits:
                each.advance()
    for copy in ig_stores:
        copy.wait()


def pixels_first(field):
    n, side, _, channels = field.shape
    return jnp.transpose(field, (1, 2, 0, 3)).reshape(side * side * n, channels)


def images_first(field, n, side):
    return jnp.transpose(field.reshape(side, side, n, field.shape[1]), (2, 0, 1, 3))


def columns_last(tiles):
    return jnp.transpose(tiles, (1, 0, 2)).reshape(tiles.shape[1], -1).astype(F32)


def per_device(
    grp,
    dp,
    image_in,
    slot_mask,
    conv_reduce,
    gain_reduce,
    bias_reduce,
    conv_group,
    gain_group,
    bias_group,
    conv_expand,
    gain_expand,
    bias_expand,
    out_grad,
):
    n, side, _, C = image_in.shape
    W = conv_reduce.shape[1]
    cg = conv_group.shape[3]
    rows = side * side * n
    dims = (n, side, C, W, grp, dp, cg)
    devices = grp * dp
    half = W // 2
    taps_rows = 9 * conv_group.shape[2]
    par1 = jnp.stack([gain_reduce, bias_reduce]).astype(F32)
    par3 = jnp.stack([gain_expand, bias_expand]).astype(F32)
    packed = jnp.concatenate(
        [
            conv_group.reshape(taps_rows, cg),
            gain_group.reshape(1, cg),
            bias_group.reshape(1, cg),
            jnp.zeros((14, cg), BF),
        ]
    )
    x = pixels_first(image_in)
    upstream = pixels_first(out_grad)
    any_spec = pl.BlockSpec(memory_space=pl.ANY)
    vmem = pl.BlockSpec(memory_space=pltpu.VMEM)
    smem = pl.BlockSpec(memory_space=pltpu.SMEM)
    sds = jax.ShapeDtypeStruct
    dma = pltpu.SemaphoreType.DMA
    blocks = W // CB
    span = rows + 2 * side * n
    parts = C // 512
    tap_units = -(-taps_rows * blocks // (16 * devices))
    stages = 2 * sum(len(bits) for bits in index_bits(grp, dp))

    def params(which):
        return pltpu.CompilerParams(
            collective_id=which, has_side_effects=True, vmem_limit_bytes=VMEM_LIMIT
        )

    red, mixed, p1, p2, wgall = pl.pallas_call(
        functools.partial(ka_kernel, dims),
        name="forward_a",
        out_shape=(
            sds((rows, W), F32),
            sds((rows, W), F32),
            sds((8, W), F32),
            sds((8, W), F32),
            sds((grp, taps_rows + 16, cg), BF),
        ),
        in_specs=[any_spec, any_spec, any_spec, vmem, smem],
        out_specs=(any_spec, any_spec, vmem, vmem, any_spec),
        scratch_shapes=[
            pltpu.VMEM((rows, C), BF),
            pltpu.VMEM((C, W), BF),
            pltpu.VMEM((rows, W), F32),
            pltpu.VMEM((rows, W), F32),
            pltpu.VMEM((grp, taps_rows + 16, cg), BF),
            pltpu.VMEM((blocks, 6 * CB, 2 * CB), BF),
            pltpu.VMEM((span, 3 * CB), BF),
            pltpu.VMEM((devices, 1, 128), F32),
            pltpu.VMEM((2, devices, 2, half), F32),
            pltpu.VMEM((2, devices, 2, half), F32),
            dma((5,)),
            dma((4,)),
            dma((2, grp - 1)),
            dma((2,)),
            dma((2, 2)),
            dma((2, 2)),
        ],
        compiler_params=params(0),
    )(x, conv_reduce, packed, par1, slot_mask)

    block_out, pre, h2g, ewg, sums3, sums2 = pl.pallas_call(
        functools.partial(kb_kernel, dims),
        name="middle_b",
        out_shape=(
            sds((rows, C), BF),
            sds((rows, C), F32),
            sds((rows, W), BF),
            sds((W, C), BF),
            sds((2, C), F32),
            sds((2, W), F32),
        ),
        in_specs=[any_spec, vmem, any_spec, any_spec, any_spec, vmem, smem],
        out_specs=(any_spec, any_spec, any_spec, any_spec, vmem, vmem),
        scratch_shapes=[
            pltpu.VMEM((rows, W), F32),
            pltpu.VMEM((W, C), BF),
            pltpu.VMEM((rows, W), BF),
            pltpu.VMEM((rows, C), F32),
            pltpu.VMEM((rows, C), BF),
            pltpu.VMEM((rows, C), BF),
            pltpu.VMEM((rows, C), BF),
            pltpu.VMEM((rows, W), BF),
            pltpu.VMEM((8, C), F32),
            pltpu.VMEM((devices, 1, 128), F32),
            pltpu.VMEM((parts, devices, 2, 512), F32),
            pltpu.VMEM((parts, devices, 2, 512), F32),
            dma((10,)),
            dma((4,)),
            dma((2,)),
            dma((2, parts)),
            dma((2, parts)),
            dma((2, 2)),
        ],
        compiler_params=params(1),
    )(mixed, p2, conv_expand, x, upstream, par3, slot_mask)

    image_grad, rwg_sum, ewg_sum, gwg_sum, sums1 = pl.pallas_call(
        functools.partial(kc_kernel, dims),
        name="backward_c",
        out_shape=(
            sds((rows, C), BF),
            sds((W * C // 128, 128), BF),
            sds((W * C // 128, 128), BF),
            sds((tap_units * 16 * devices, 128), BF),
            sds((2, W), F32),
        ),
        in_specs=[any_spec] * 3 + [vmem] * 4 + [any_spec] * 4 + [smem],
        out_specs=(any_spec, any_spec, any_spec, any_spec, vmem),
        scratch_shapes=[
            pltpu.VMEM((rows, W), BF),
            pltpu.VMEM((rows, W), F32),
            pltpu.VMEM((rows, W), F32),
            pltpu.VMEM((rows, C), BF),
            pltpu.VMEM((C, W), BF),
            pltpu.VMEM((2, rows // 2, 512), F32),
            pltpu.VMEM((W * C // 128, 128), BF),
            pltpu.VMEM((W * C // 128, 128), BF),
            pltpu.VMEM((W * C // 128, 128), BF),
            pltpu.VMEM((W * C // 128, 128), BF),
            pltpu.VMEM((tap_units * 16 * devices, 128), BF),
            pltpu.VMEM((tap_units * 16 * devices, 128), BF),
            pltpu.VMEM((blocks, 2 * CB, 6 * CB), BF),
            pltpu.VMEM((span, 3 * CB), BF),
            pltpu.VMEM((span, CB), BF),
            pltpu.VMEM((8, W), F32),
            pltpu.VMEM((2, devices, 2, half), F32),
            dma((3, blocks)),
            dma((4 + C // 128,)),
            dma((C // 512,)),
            dma((2, 2)),
            dma((2, 3, stages)),
            dma((2, 2, 3, stages)),
            dma((2, 3, stages)),
            dma((4, 3)),
        ],
        compiler_params=params(2),
    )(h2g, mixed, red, p1, p2, sums2, wgall, x, conv_reduce, pre, ewg, slot_mask)

    shard = cg // CB
    gwg_sum = gwg_sum[: taps_rows * blocks].reshape(blocks, taps_rows, CB)
    gwg_sum = lax.dynamic_slice_in_dim(gwg_sum, lax.axis_index("grp") * shard, shard, 0)
    group_wgrad = columns_last(gwg_sum)
    own = lax.dynamic_slice_in_dim(sums2, lax.axis_index("grp") * cg, cg, 1)
    return (
        images_first(block_out, n, side),
        images_first(image_grad, n, side),
        columns_last(rwg_sum.reshape(W // 128, C, 128)),
        sums1[0],
        sums1[1],
        group_wgrad.reshape(conv_group.shape),
        own[0],
        own[1],
        columns_last(ewg_sum.reshape(C // 128, W, 128)),
        sums3[0],
        sums3[1],
    )


def solution(mesh):
    placed = (
        P(("grp", "dp"), None, None, None),
        P(("grp", "dp")),
        P(),
        P(),
        P(),
        P(None, None, None, "grp"),
        P("grp"),
        P("grp"),
        P(),
        P(),
        P(),
        P(("grp", "dp"), None, None, None),
    )
    return jax.shard_map(
        functools.partial(per_device, mesh.shape["grp"], mesh.shape["dp"]),
        mesh=mesh,
        in_specs=placed,
        out_specs=(
            P(("grp", "dp"), None, None, None),
            P(("grp", "dp"), None, None, None),
            P(),
            P(),
            P(),
            P(None, None, None, "grp"),
            P("grp"),
            P("grp"),
            P(),
            P(),
            P(),
        ),
        check_vma=False,
    )
```

```python
import functools

import jax
import jax.numpy as jnp
from jax import lax
from jax.experimental import pallas as pl
from jax.experimental.pallas import tpu as pltpu
from jax.sharding import PartitionSpec as P

EPS = 1e-05
BF = jnp.bfloat16
F32 = jnp.float32
MESH = pl.DeviceIdType.MESH
CB = 128
VMEM_LIMIT = 61952 * 1024


def aligned(index, size):
    return pl.ds(pl.multiple_of(index * size, size), size)


def sigmoid(values):
    return 0.5 * jnp.tanh(0.5 * values) + 0.5


def fold(values, images):
    rows, cols = values.shape
    return jnp.sum(values.reshape(rows // images, images, cols), axis=0)


def down(values):
    return jnp.sum(values, axis=0, keepdims=True)


def spread_rows(values, row):
    rows, cols = values.shape
    images = row.shape[0]
    return (values.reshape(rows // images, images, cols) * wide(row, cols)[None]).reshape(rows, cols)


class Links:
    def __init__(self, grp, dp):
        self.grp, self.dp = grp, dp
        self.count = grp * dp
        self.g, self.d = lax.axis_index("grp"), lax.axis_index("dp")
        self.me = self.g * dp + self.d

    def peer(self, step):
        target = lax.rem(self.me + step, self.count)
        return (target // self.dp, lax.rem(target, self.dp))

    def greet(self):
        barrier = pltpu.get_barrier_semaphore()

        @pl.loop(1, self.count)
        def _(step):
            pl.semaphore_signal(barrier, inc=1, device_id=self.peer(step), device_id_type=MESH)

    def greeted(self):
        pl.semaphore_wait(pltpu.get_barrier_semaphore(), self.count - 1)

    def send(self, buf, send_sem, recv_sem):
        @pl.loop(1, self.count)
        def _(step):
            pltpu.make_async_remote_copy(
                src_ref=buf.at[self.me],
                dst_ref=buf.at[self.me],
                send_sem=send_sem,
                recv_sem=recv_sem,
                device_id=self.peer(step),
                device_id_type=MESH,
            ).start()

    def wait(self, buf, send_sem, recv_sem):
        others = buf.at[pl.ds(0, self.count - 1)]
        copy = pltpu.make_async_remote_copy(
            src_ref=others,
            dst_ref=others,
            send_sem=send_sem,
            recv_sem=recv_sem,
            device_id=self.peer(1),
            device_id_type=MESH,
        )
        copy.wait_recv()
        copy.wait_send()


def index_bits(grp, dp):
    ones = lambda count: [1 << k for k in range(count.bit_length() - 1)]
    g_bits = [("grp", w) for w in ones(grp)]
    d_bits = [("dp", w) for w in ones(dp)]
    low = len(d_bits) // 2
    return g_bits[:1], g_bits[1:], d_bits[:low], d_bits[low:]


class Reduction:
    def __init__(self, links, buf, recv, out, sems, own_sems):
        self.links, self.buf, self.recv, self.out = links, buf, recv, out
        self.sems, self.own_sems = sems, own_sems
        core, y, x, z = index_bits(links.grp, links.dp)
        orders = (core + x + y + z, core + y + x + z, core + z + x + y)
        unit = 16 * links.count
        units = buf.shape[0] // unit
        last = units // 4
        sizes = ((units - last + 1) // 2, (units - last) // 2, last)
        self.parts = []
        start = 0
        for order, size in zip(orders, sizes):
            if size:
                self.parts.append(dict(start=start, size=size * unit, lo=start, order=order))
            start += size * unit
        self.bits = len(orders[0])
        self.stage = 0
        self.started = False

    def place(self, bit):
        axis, weight = bit
        at = self.links.g if axis == "grp" else self.links.d
        value = lax.rem(at // weight, 2)
        other = at + weight * (1 - 2 * value)
        return value, (other, self.links.d) if axis == "grp" else (self.links.g, other)

    def copy(self, index, part):
        rows = lambda lo, size: pl.ds(pl.multiple_of(lo, 16), size)
        halving = self.stage < self.bits
        bit = part["order"][self.stage if halving else 2 * self.bits - 1 - self.stage]
        value, device = self.place(bit)
        if halving:
            half = part["size"] // 2
            src = self.buf.at[rows(part["lo"] + (1 - value) * half, half)]
            dst = self.recv.at[rows(part["start"], half)]
        else:
            here = self.buf if self.stage == self.bits else self.out
            src = here.at[rows(part["lo"], part["size"])]
            dst = self.out.at[rows(part["lo"], part["size"])]
        return value, pltpu.make_async_remote_copy(
            src_ref=src,
            dst_ref=dst,
            send_sem=self.sems.at[0, index, self.stage],
            recv_sem=self.sems.at[1, index, self.stage],
            device_id=device,
            device_id_type=MESH,
        )

    def start(self, now=0.0):
        self.started = True
        for index, part in enumerate(self.parts):
            self.copy(index, part)[1].start()
        self.ready = now + self.estimate()

    def estimate(self):
        halving = self.stage < self.bits
        longest = 0.0
        for part in self.parts:
            kilobytes = (part["size"] // 2 if halving else part["size"]) * 0.256
            near = self.stage in (0, 2 * self.bits - 1)
            longest = max(longest, 1.5 + kilobytes / 500 if near else 3.0 + kilobytes / 35)
        return longest

    def advance(self, now=0.0):
        for index, part in enumerate(self.parts):
            value, copy = self.copy(index, part)
            copy.wait()
            if self.stage < self.bits:
                half = part["size"] // 2
                keep, base = part["lo"] + value * half, part["start"]
                chunk = max(c for c in range(16, 513, 16) if half % c == 0)

                @pl.loop(0, half // chunk)
                def _(k):
                    at = pl.ds(pl.multiple_of(keep + k * chunk, 16), chunk)
                    more = self.recv[pl.ds(pl.multiple_of(base + k * chunk, 16), chunk), :]
                    self.buf[at, :] = (self.buf[at, :].astype(F32) + more.astype(F32)).astype(BF)

                part.update(lo=keep, size=half, start=base + half)
                if self.stage == self.bits - 1:
                    at = pl.ds(pl.multiple_of(keep, 16), half)
                    part["own"] = pltpu.make_async_copy(
                        self.buf.at[at], self.out.at[at], self.own_sems.at[index]
                    )
                    part["own"].start()
            else:
                if self.stage == self.bits:
                    part["own"].wait()
                part.update(lo=part["lo"] - value * part["size"], size=2 * part["size"])
            if self.stage + 1 < 2 * self.bits:
                self.stage += 1
                self.copy(index, part)[1].start()
                self.stage -= 1
        self.stage += 1
        self.ready = now + self.estimate()

    def busy(self):
        return self.started and self.stage < 2 * self.bits


class Clock:
    def __init__(self, reductions):
        self.now, self.reductions = 0.0, reductions

    def spend(self, microseconds):
        self.now += microseconds
        for each in self.reductions:
            if each.busy() and each.ready <= self.now:
                each.advance(self.now)

    def finish(self):
        while any(each.busy() for each in self.reductions):
            first = min((e for e in self.reductions if e.busy()), key=lambda e: e.ready)
            self.now = max(self.now, first.ready)
            first.advance(self.now)


def wide(row, cols):
    return jnp.concatenate([row] * (cols // 128), axis=-1)


def row_weights(mask_ref, images):
    at = lax.broadcasted_iota(jnp.int32, (images, 128), 0)
    column = jnp.zeros((images, 128), F32)
    count = jnp.float32(0.0)
    for i in range(images):
        value = mask_ref[i].astype(F32)
        column = jnp.where(at == i, value, column)
        count = count + value
    return column, count


def merge_stats(buf, counts, cols):
    each = wide(counts, cols)
    total = jnp.sum(each, axis=0)
    parts = buf[...]
    means, squares = parts[:, 0:1], parts[:, 1:2]
    average = jnp.sum(each * means, axis=0) / total
    gap = means - average
    spread = jnp.sum(squares + each * gap * gap, axis=0) / total
    return average, lax.rsqrt(spread + EPS)


def dense_taps(shard):
    group = 32
    row = lax.broadcasted_iota(jnp.int32, (CB, CB), 0) // group
    col = lax.broadcasted_iota(jnp.int32, (CB, CB), 1) // group
    keep = row == col
    zero = jnp.zeros((CB, CB), BF)

    def block(row_tap, col_tap):
        start = (row_tap * 3 + col_tap) * group
        tile = shard(start, group).astype(F32)
        full = jnp.concatenate([tile] * (CB // group), axis=0)
        return jnp.where(keep, full, 0.0).astype(BF)

    return block, zero


def shifted(values, images):
    edge = jnp.zeros((images, values.shape[1]), F32)
    return (
        jnp.concatenate([edge, values[:-images]], axis=0),
        jnp.concatenate([values[images:], edge], axis=0),
    )


def local_stats(field, cols, mean_of, rows, chunk, images, row, inverse, width):
    mean = down(mean_of * wide(row, width)) * wide(inverse, width)

    def body(k, acc):
        gap = field[aligned(k, chunk), cols] - mean
        return acc + fold(gap * gap, images)

    squares = lax.fori_loop(0, rows // chunk, body, jnp.zeros((images, width), F32))
    return mean, down(squares * wide(row, width))


def ka_kernel(
    dims,
    x_hbm,
    wr_hbm,
    wg_hbm,
    par_ref,
    mask_ref,
    red_hbm,
    mixed_hbm,
    p1_ref,
    p2_ref,
    wgall_hbm,
    xv,
    wr,
    red,
    mixed,
    wgall,
    taps,
    hbuf,
    cnt,
    ex1,
    ex2,
    load_sem,
    store_sem,
    gather_sem,
    cnt_sem,
    ex1_sem,
    ex2_sem,
):
    n, side, C, W, grp, dp, cg = dims
    rows = side * side * n
    line = side * n
    half = W // 2
    tile = rows // 2
    links = Links(grp, dp)
    links.greet()
    w_loads = [
        pltpu.make_async_copy(
            wr_hbm.at[:, pl.ds(h * half, half)], wr.at[:, pl.ds(h * half, half)], load_sem.at[h]
        )
        for h in range(2)
    ]
    x_loads = [
        pltpu.make_async_copy(
            x_hbm.at[pl.ds(h * tile, tile), :], xv.at[pl.ds(h * tile, tile), :], load_sem.at[2 + h]
        )
        for h in range(2)
    ]
    w_loads[0].start()
    x_loads[0].start()
    x_loads[1].start()
    w_loads[1].start()
    own = pltpu.make_async_copy(wg_hbm, wgall.at[links.g], load_sem.at[4])
    own.start()

    row, valid = row_weights(mask_ref, n)
    local = jnp.full((1, 128), 1.0, F32) * (valid * float(side * side))
    cnt[links.me] = local
    inverse = 1.0 / jnp.maximum(local, 1.0)
    hbuf[...] = jnp.zeros(hbuf.shape, BF)
    links.greeted()
    links.send(cnt, cnt_sem.at[0], cnt_sem.at[1])
    gathers = []
    for k in range(1, grp):
        copy = pltpu.make_async_remote_copy(
            src_ref=wg_hbm,
            dst_ref=wgall.at[links.g],
            send_sem=gather_sem.at[0, k - 1],
            recv_sem=gather_sem.at[1, k - 1],
            device_id=(lax.rem(links.g + k, grp), links.d),
            device_id_type=MESH,
        )
        copy.start()
        gathers.append(copy)

    for h in range(2):
        w_loads[h].wait()
        cols = pl.ds(h * half, half)
        total = jnp.zeros((n, half), F32)
        for t in range(2):
            if h == 0:
                x_loads[t].wait()
            at = pl.ds(t * tile, tile)
            out = jnp.dot(xv[at, :], wr[:, cols], preferred_element_type=F32)
            red[at, cols] = out
            total += fold(out, n)
        mean, squares = local_stats(red, cols, total, rows, line, n, row, inverse, half)
        ex1[h, links.me, 0:1, :] = mean
        ex1[h, links.me, 1:2, :] = squares
        if h == 0:
            links.wait(cnt, cnt_sem.at[0], cnt_sem.at[1])
        links.send(ex1.at[h], ex1_sem.at[0, h], ex1_sem.at[1, h])
    red_store = pltpu.make_async_copy(red, red_hbm, store_sem.at[0])
    red_store.start()

    own.wait()
    for copy in gathers:
        copy.wait()
    store_wg = pltpu.make_async_copy(wgall, wgall_hbm, store_sem.at[1])
    store_wg.start()
    blocks = W // CB
    per_shard = cg // CB

    @pl.loop(0, blocks)
    def _(b):
        shard_at, lane = b // per_shard, aligned(lax.rem(b, per_shard), CB)
        block, zero = dense_taps(lambda start, size: wgall[shard_at, pl.ds(start, size), lane])
        for dx in range(3):
            taps[b, pl.ds(dx * CB, CB), 0:CB] = block(0, dx)
            taps[b, pl.ds(dx * CB, CB), CB : 2 * CB] = zero
            taps[b, pl.ds((3 + dx) * CB, CB), 0:CB] = block(1, dx)
            taps[b, pl.ds((3 + dx) * CB, CB), CB : 2 * CB] = block(2, dx)

    for h in range(2):
        links.wait(ex1.at[h], ex1_sem.at[0, h], ex1_sem.at[1, h])
        cols = pl.ds(h * half, half)
        average, scale = merge_stats(ex1.at[h], cnt[...], half)
        p1_ref[0:1, cols] = average
        p1_ref[1:2, cols] = scale

        @pl.loop(h * blocks // 2, (h + 1) * blocks // 2)
        def _(b):
            lanes = aligned(b, CB)
            mean, rstd = p1_ref[0:1, lanes], p1_ref[1:2, lanes]
            gain, shift = par_ref[0:1, lanes], par_ref[1:2, lanes]

            @pl.loop(0, side)
            def _(r):
                act = (red[aligned(r, line), lanes] - mean) * rstd * gain + shift
                hidden = act * sigmoid(act)
                left, right = shifted(hidden, n)
                to = aligned(r + 1, line)
                hbuf[to, 0:CB] = left.astype(BF)
                hbuf[to, CB : 2 * CB] = hidden.astype(BF)
                hbuf[to, 2 * CB : 3 * CB] = right.astype(BF)

            lhs = jnp.concatenate([hbuf[0 : rows + line, :], hbuf[line : rows + 2 * line, :]], axis=1)
            out = jnp.dot(lhs, taps[b], preferred_element_type=F32)
            field = out[0:rows, 0:CB] + out[line : line + rows, CB:]
            mixed[:, lanes] = field
            mean, squares = local_stats(
                mixed, lanes, fold(field, n), rows, line, n, row, inverse, CB
            )
            inner = aligned(lax.rem(b, blocks // 2), CB)
            ex2[h, links.me, 0:1, inner] = mean
            ex2[h, links.me, 1:2, inner] = squares

        links.send(ex2.at[h], ex2_sem.at[0, h], ex2_sem.at[1, h])
        pltpu.make_async_copy(mixed.at[:, cols], mixed_hbm.at[:, cols], store_sem.at[2 + h]).start()

    count = jnp.sum(wide(cnt[...], W), axis=0)
    p1_ref[2:3, :] = count
    p2_ref[2:3, :] = count
    extra = jnp.concatenate(
        [wgall[k, pl.ds(9 * 32, 16), :].astype(F32) for k in range(grp)], axis=1
    )
    p2_ref[3:5, :] = extra[0:2]
    p1_ref[3:5, :] = par_ref[0:2, :]
    for h in range(2):
        links.wait(ex2.at[h], ex2_sem.at[0, h], ex2_sem.at[1, h])
        cols = pl.ds(h * half, half)
        average, scale = merge_stats(ex2.at[h], cnt[...], half)
        p2_ref[0:1, cols] = average
        p2_ref[1:2, cols] = scale
    red_store.wait()
    store_wg.wait()
    for h in range(2):
        cols = pl.ds(h * half, half)
        pltpu.make_async_copy(mixed.at[:, cols], mixed_hbm.at[:, cols], store_sem.at[2 + h]).wait()


def kb_kernel(
    dims,
    mixed_hbm,
    p2_ref,
    we_hbm,
    x_hbm,
    dout_hbm,
    par_ref,
    mask_ref,
    out_hbm,
    pre_hbm,
    ein_hbm,
    h2_hbm,
    sums3_ref,
    mixed,
    we,
    h2,
    expd,
    xe,
    dout,
    n3,
    stat3,
    cnt,
    ex3,
    ex4,
    load_sem,
    store_sem,
    cnt_sem,
    ex3_sem,
    ex4_sem,
):
    n, side, C, W, grp, dp, cg = dims
    rows = side * side * n
    line = side * n
    tile = rows // 2
    links = Links(grp, dp)
    links.greet()
    part_cols = 512
    parts = C // part_cols
    pieces = 7
    piece = rows // pieces
    m_loads = [
        pltpu.make_async_copy(
            mixed_hbm.at[pl.ds(k * piece, piece), :],
            mixed.at[pl.ds(k * piece, piece), :],
            load_sem.at[k],
        )
        for k in range(pieces)
    ]
    for copy in m_loads:
        copy.start()
    we_load = pltpu.make_async_copy(we_hbm, we, load_sem.at[pieces])
    we_load.start()
    x_load = pltpu.make_async_copy(x_hbm, xe, load_sem.at[pieces + 1])
    x_load.start()
    d_load = pltpu.make_async_copy(dout_hbm, dout, load_sem.at[pieces + 2])
    d_load.start()
    row, valid = row_weights(mask_ref, n)
    local = jnp.full((1, 128), 1.0, F32) * (valid * float(side * side))
    cnt[links.me] = local
    inverse = 1.0 / jnp.maximum(local, 1.0)
    links.greeted()
    links.send(cnt, cnt_sem.at[0], cnt_sem.at[1])

    step = 256
    lines = rows // line
    for k in range(pieces):
        m_loads[k].wait()

        @pl.loop(k * lines // pieces, (k + 1) * lines // pieces)
        def _(r):
            at = aligned(r, line)
            for q in range(W // step):
                lanes = pl.ds(q * step, step)
                normed = (mixed[at, lanes] - p2_ref[0:1, lanes]) * p2_ref[1:2, lanes]
                act = normed * p2_ref[3:4, lanes] + p2_ref[4:5, lanes]
                h2[at, lanes] = (act * sigmoid(act)).astype(BF)

    h2_store = pltpu.make_async_copy(h2, h2_hbm, store_sem.at[2])
    h2_store.start()

    we_load.wait()
    links.wait(cnt, cnt_sem.at[0], cnt_sem.at[1])
    for part in range(parts):
        cols = pl.ds(part * part_cols, part_cols)
        total = jnp.zeros((n, part_cols), F32)
        for t in range(2):
            at = pl.ds(t * tile, tile)
            out = jnp.dot(h2[at, :], we[:, cols], preferred_element_type=F32)
            expd[at, cols] = out
            total += fold(out, n)
        mean, squares = local_stats(expd, cols, total, rows, line, n, row, inverse, part_cols)
        ex3[part, links.me, 0:1, :] = mean
        ex3[part, links.me, 1:2, :] = squares
        links.send(ex3.at[part], ex3_sem.at[0, part], ex3_sem.at[1, part])

    x_load.wait()
    d_load.wait()
    step = 128
    for part in range(parts):
        cols = pl.ds(part * part_cols, part_cols)
        links.wait(ex3.at[part], ex3_sem.at[0, part], ex3_sem.at[1, part])
        average, scale = merge_stats(ex3.at[part], cnt[...], part_cols)
        stat3[0:1, cols] = average
        stat3[1:2, cols] = scale

        @pl.loop(0, part_cols // step)
        def _(q):
            lanes = pl.ds(pl.multiple_of(part * part_cols + q * step, step), step)
            mean, rstd = stat3[0:1, lanes], stat3[1:2, lanes]
            gain, shift = par_ref[0:1, lanes], par_ref[1:2, lanes]

            def body(r, sums):
                at = aligned(r, line)
                normed = (expd[at, lanes] - mean) * rstd
                summed = normed * gain + shift + xe[at, lanes].astype(F32)
                sig = sigmoid(summed)
                silu = summed * sig
                grad = spread_rows(dout[at, lanes].astype(F32), row) * (sig + silu * (1.0 - sig))
                dout[at, lanes] = spread_rows(silu, row).astype(BF)
                expd[at, lanes] = grad
                n3[at, lanes] = normed.astype(BF)
                return sums[0] + fold(grad * normed, n), sums[1] + fold(grad, n)

            zeros = jnp.zeros((n, step), F32)
            gain_sum, shift_sum = lax.fori_loop(0, lines, body, (zeros, zeros))
            inner = aligned(q, step)
            ex4[part, links.me, 0:1, inner] = down(gain_sum)
            ex4[part, links.me, 1:2, inner] = down(shift_sum)

        links.send(ex4.at[part], ex4_sem.at[0, part], ex4_sem.at[1, part])
    out_store = pltpu.make_async_copy(dout, out_hbm, store_sem.at[0])
    out_store.start()
    pre_store = pltpu.make_async_copy(expd, pre_hbm, store_sem.at[1])
    pre_store.start()

    total = jnp.sum(wide(cnt[...], part_cols), axis=0)
    ein_stores = []
    for part in range(parts):
        cols = pl.ds(part * part_cols, part_cols)
        links.wait(ex4.at[part], ex4_sem.at[0, part], ex4_sem.at[1, part])
        sums = jnp.sum(ex4[part], axis=0)
        sums3_ref[0:2, cols] = sums
        stat3[2:3, cols] = sums[0:1] / total
        stat3[3:4, cols] = sums[1:2] / total
        stat3[4:5, cols] = par_ref[0:1, cols] * stat3[1:2, cols]

        @pl.loop(0, lines)
        def _(r):
            at = aligned(r, line)
            for q in range(part_cols // step):
                lanes = pl.ds(part * part_cols + q * step, step)
                off = stat3[3:4, lanes] + n3[at, lanes].astype(F32) * stat3[2:3, lanes]
                value = stat3[4:5, lanes] * (expd[at, lanes] - spread_rows(off, row))
                xe[at, lanes] = value.astype(BF)
        store = pltpu.make_async_copy(xe.at[:, cols], ein_hbm.at[:, cols], store_sem.at[3 + part])
        store.start()
        ein_stores.append(store)
    h2_store.wait()
    out_store.wait()
    pre_store.wait()
    for store in ein_stores:
        store.wait()


def kc_kernel(
    dims,
    mixed_hbm,
    red_hbm,
    ein_hbm,
    h2_hbm,
    we_hbm,
    p1_ref,
    p2_ref,
    wgall_ref,
    x_hbm,
    wr_hbm,
    pre_hbm,
    mask_ref,
    ig_hbm,
    rwg_hbm,
    ewg_hbm,
    gwg_hbm,
    sums1_ref,
    sums2_ref,
    h2,
    h2g,
    mixed,
    red,
    xv,
    weight,
    pre,
    ewg,
    ewg_in,
    rwg,
    rwg_in,
    gwg,
    gwg_in,
    taps,
    dbuf,
    hbuf,
    coef,
    ex5,
    ex6,
    load_sem,
    pre_sem,
    store_sem,
    ex5_sem,
    ex6_sem,
    ewg_sem,
    rwg_sem,
    gwg_sem,
    own_sem,
):
    n, side, C, W, grp, dp, cg = dims
    rows = side * side * n
    line = side * n
    half = W // 2
    tile = rows // 2
    blocks = W // CB
    per_shard = cg // CB
    part_cols = 512
    parts = C // part_cols
    group = 32
    links = Links(grp, dp)
    links.greet()

    used = []

    def load(src, dst):
        copy = pltpu.make_async_copy(src, dst, load_sem.at[len(used)])
        used.append(copy)
        copy.start()
        return copy

    column = lambda k, width: pl.ds(k * width, width)
    h2_load = load(h2_hbm, h2)
    ein_loads = [
        load(ein_hbm.at[:, column(k, part_cols)], xv.at[:, column(k, part_cols)])
        for k in range(parts)
    ]
    we_loads = [load(we_hbm.at[:, column(k, W)], weight.at[k]) for k in range(C // W)]
    mixed_loads = [
        load(mixed_hbm.at[:, column(h, half)], mixed.at[:, column(h, half)]) for h in range(2)
    ]
    red_loads = [load(red_hbm.at[:, column(h, half)], red.at[:, column(h, half)]) for h in range(2)]
    pre_loads = [
        pltpu.make_async_copy(
            pre_hbm.at[pl.ds(t * tile, tile), column(part, part_cols)], pre.at[t], pre_sem.at[t]
        )
        for part in range(parts)
        for t in range(2)
    ]
    pre_loads[0].start()
    pre_loads[1].start()
    half_rows = half // 128 * C
    pick = lambda h, refs: [ref.at[pl.ds(h * half_rows, half_rows)] for ref in refs]
    expand_sums = [
        Reduction(links, *pick(h, (ewg, ewg_in, ewg_hbm)), ewg_sem.at[h], own_sem.at[h])
        for h in range(2)
    ]
    reduce_sums = [
        Reduction(links, *pick(h, (rwg, rwg_in, rwg_hbm)), rwg_sem.at[h], own_sem.at[2 + h])
        for h in range(2)
    ]
    group_sum = Reduction(links, gwg, gwg_in, gwg_hbm, gwg_sem, own_sem.at[4])
    clock = Clock(expand_sums + reduce_sums + [group_sum])
    gwg[...] = jnp.zeros(gwg.shape, BF)
    row, valid = row_weights(mask_ref, n)
    dbuf[...] = jnp.zeros(dbuf.shape, BF)
    hbuf[...] = jnp.zeros(hbuf.shape, BF)
    total = p2_ref[2:3, 0:half]
    keep = (
        lax.broadcasted_iota(jnp.int32, (CB, CB), 0) // group
        == lax.broadcasted_iota(jnp.int32, (CB, CB), 1) // group
    )
    transposed = (((0,), (0,)), ((), ()))
    rowwise = (((1,), (1,)), ((), ()))

    h2_load.wait()
    for part in range(parts):
        ein_loads[part].wait()
        out = lax.dot_general(
            h2[...], xv[:, column(part, part_cols)], transposed, preferred_element_type=F32
        )
        for q in range(part_cols // 128):
            at = pl.ds((part * (part_cols // 128) + q) * W, W)
            ewg[at, :] = out[:, q * 128 : (q + 1) * 128].astype(BF)
        if part == 0:
            links.greeted()
        clock.spend(2.3)
        if part % 2:
            expand_sums[part // 2].start(clock.now)

    for copy in we_loads:
        copy.wait()
    step = CB
    for h in range(2):
        cols = column(h, half)
        both = jnp.concatenate([weight[k, cols, :] for k in range(C // W)], axis=1)
        for t in range(2):
            at = pl.ds(t * tile, tile)
            h2g[at, cols] = lax.dot_general(
                xv[at, :], both, rowwise, preferred_element_type=F32
            ).astype(BF)
            clock.spend(2.4)
        mixed_loads[h].wait()

        @pl.loop(0, half // step)
        def _(q):
            lanes = pl.ds(pl.multiple_of(h * half + q * step, step), step)
            mean, rstd = p2_ref[0:1, lanes], p2_ref[1:2, lanes]
            gain, shift = p2_ref[3:4, lanes], p2_ref[4:5, lanes]

            def body(r, sums):
                at = aligned(r, line)
                normed = (mixed[at, lanes] - mean) * rstd
                act = normed * gain + shift
                sig = sigmoid(act)
                grad = h2g[at, lanes].astype(F32) * (sig + act * sig * (1.0 - sig))
                return sums[0] + fold(grad * normed, n), sums[1] + fold(grad, n)

            zeros = jnp.zeros((n, step), F32)
            gain_sum, shift_sum = lax.fori_loop(0, side, body, (zeros, zeros))
            inner = aligned(q, step)
            ex5[h, links.me, 0:1, inner] = down(gain_sum)
            ex5[h, links.me, 1:2, inner] = down(shift_sum)

        links.send(ex5.at[h], ex5_sem.at[0, h], ex5_sem.at[1, h])
        clock.spend(2.0)
    x_load = load(x_hbm, xv)
    wr_loads = [load(wr_hbm.at[column(k, W), :], weight.at[k]) for k in range(C // W)]

    def second_sums(h):
        cols = column(h, half)
        links.wait(ex5.at[h], ex5_sem.at[0, h], ex5_sem.at[1, h])
        sums = jnp.sum(ex5[h], axis=0)
        sums2_ref[0:2, cols] = sums
        coef[0:1, cols] = sums[0:1] / total
        coef[1:2, cols] = sums[1:2] / total
        coef[2:3, cols] = p2_ref[3:4, cols] * p2_ref[1:2, cols]
        red_loads[h].wait()

    def conv_block(h, b):
        shard_at, lane = b // per_shard, pl.ds(b % per_shard * CB, CB)
        block, zero = dense_taps(lambda start, size: wgall_ref[shard_at, pl.ds(start, size), lane])
        for dx in range(3):
            taps[0:CB, pl.ds(dx * CB, CB)] = block(2, 2 - dx)
            taps[CB : 2 * CB, pl.ds(dx * CB, CB)] = zero
            taps[0:CB, pl.ds((3 + dx) * CB, CB)] = block(1, 2 - dx)
            taps[CB : 2 * CB, pl.ds((3 + dx) * CB, CB)] = block(0, 2 - dx)
        lanes = pl.ds(b * CB, CB)

        @pl.loop(0, side)
        def _(r):
            at = aligned(r, line)
            normed = (mixed[at, lanes] - p2_ref[0:1, lanes]) * p2_ref[1:2, lanes]
            act = normed * p2_ref[3:4, lanes] + p2_ref[4:5, lanes]
            sig = sigmoid(act)
            grad = h2g[at, lanes].astype(F32) * (sig + act * sig * (1.0 - sig))
            off = coef[1:2, lanes] + normed * coef[0:1, lanes]
            grad = coef[2:3, lanes] * (grad - spread_rows(off, row))
            left, right = shifted(grad, n)
            to = aligned(r + 1, line)
            dbuf[to, 0:CB] = left.astype(BF)
            dbuf[to, CB : 2 * CB] = grad.astype(BF)
            dbuf[to, 2 * CB : 3 * CB] = right.astype(BF)

        lhs = jnp.concatenate([dbuf[0 : rows + line, :], dbuf[line : rows + 2 * line, :]], axis=1)
        out = lax.dot_general(lhs, taps[...], rowwise, preferred_element_type=F32)
        mixed[:, lanes] = out[0:rows, 0:CB] + out[line : line + rows, CB:]
        mean, rstd = p1_ref[0:1, lanes], p1_ref[1:2, lanes]
        gain, shift = p1_ref[3:4, lanes], p1_ref[4:5, lanes]

        def body(r, sums):
            at = aligned(r, line)
            normed = (red[at, lanes] - mean) * rstd
            act = normed * gain + shift
            sig = sigmoid(act)
            silu = act * sig
            hbuf[aligned(r + 1, line), :] = silu.astype(BF)
            grad = mixed[at, lanes].astype(BF).astype(F32) * (sig + silu * (1.0 - sig))
            mixed[at, lanes] = grad
            return sums[0] + fold(grad * normed, n), sums[1] + fold(grad, n)

        zeros = jnp.zeros((n, CB), F32)
        gain_sum, shift_sum = lax.fori_loop(0, side, body, (zeros, zeros))
        inner = pl.ds(b % (blocks // 2) * CB, CB)
        ex6[h, links.me, 0:1, inner] = down(gain_sum)
        ex6[h, links.me, 1:2, inner] = down(shift_sum)
        clock.spend(3.3)

    def conv_wgrad(b):
        span = rows + line
        left = jnp.concatenate([hbuf[0:span, :], hbuf[line : line + span, :]], axis=1)
        right = jnp.concatenate([dbuf[0:span, :], dbuf[line : line + span, :]], axis=1)
        full = lax.dot_general(left, right, transposed, preferred_element_type=F32)
        for dy in range(3):
            left_at, right_at = ((0, 1), (0, 0), (1, 0))[dy]
            for dx in range(3):
                lane_at = (3 * right_at + 2 - dx) * CB
                part = full[left_at * CB : (left_at + 1) * CB, lane_at : lane_at + CB]
                part = jnp.where(keep, part, 0.0)
                picked = functools.reduce(
                    lambda a, b: a + b,
                    [part[k * group : (k + 1) * group] for k in range(CB // group)],
                )
                gwg[pl.ds((b * 9 + dy * 3 + dx) * group, group), :] = picked.astype(BF)
        clock.spend(1.5)

    def reduce_half(h):
        cols = column(h, half)
        links.wait(ex6.at[h], ex6_sem.at[0, h], ex6_sem.at[1, h])
        sums = jnp.sum(ex6[h], axis=0)
        sums1_ref[0:2, cols] = sums
        coef[3:4, cols] = sums[0:1] / total
        coef[4:5, cols] = sums[1:2] / total
        coef[5:6, cols] = p1_ref[3:4, cols] * p1_ref[1:2, cols]

        @pl.loop(0, side)
        def _(r):
            at = aligned(r, line)
            for q in range(half // CB):
                lanes = pl.ds(h * half + q * CB, CB)
                normed = (red[at, lanes] - p1_ref[0:1, lanes]) * p1_ref[1:2, lanes]
                off = coef[4:5, lanes] + normed * coef[3:4, lanes]
                grad = coef[5:6, lanes] * (mixed[at, lanes] - spread_rows(off, row))
                h2g[at, lanes] = grad.astype(BF)

        clock.spend(1.5)
        if h == 0:
            x_load.wait()
        big = C // 2
        for k in range(2):
            out = lax.dot_general(
                xv[:, column(k, big)], h2g[:, cols], transposed, preferred_element_type=F32
            )
            for q in range(half // 128):
                start = (h * (half // 128) + q) * C + k * big
                rwg[pl.ds(start, big), :] = out[:, q * 128 : (q + 1) * 128].astype(BF)
            clock.spend(2.2)
        reduce_sums[h].start(clock.now)

    for b in range(blocks):
        h, first, last = b * 2 // blocks, b % (blocks // 2) == 0, (b + 1) % (blocks // 2) == 0
        if first:
            second_sums(h)
        conv_block(h, b)
        if last:
            links.send(ex6.at[h], ex6_sem.at[0, h], ex6_sem.at[1, h])
        conv_wgrad(b)
        if b == blocks // 2:
            reduce_half(0)
    group_sum.start(clock.now)
    reduce_half(1)

    for copy in wr_loads:
        copy.wait()
    ig_stores = []
    for part in range(parts):
        cols = column(part, part_cols)
        for t in range(2):
            at = pl.ds(t * tile, tile)
            across = part * part_cols
            out = lax.dot_general(
                h2g[at, :],
                weight[across // W, pl.ds(across % W, part_cols), :],
                rowwise,
                preferred_element_type=F32,
            )
            pre_loads[2 * part + t].wait()
            xv[at, cols] = (out + pre[t]).astype(BF)
            if 2 * part + t + 2 < len(pre_loads):
                pre_loads[2 * part + t + 2].start()
            clock.spend(1.2)
        store = pltpu.make_async_copy(xv.at[:, cols], ig_hbm.at[:, cols], store_sem.at[part])
        store.start()
        ig_stores.append(store)
    clock.finish()
    for copy in ig_stores:
        copy.wait()


def pixels_first(field):
    n, side, _, channels = field.shape
    return jnp.transpose(field, (1, 2, 0, 3)).reshape(side * side * n, channels)


def images_first(field, n, side):
    return jnp.transpose(field.reshape(side, side, n, field.shape[1]), (2, 0, 1, 3))


def columns_last(tiles):
    return jnp.transpose(tiles, (1, 0, 2)).reshape(tiles.shape[1], -1).astype(F32)


def per_device(
    grp,
    dp,
    image_in,
    slot_mask,
    conv_reduce,
    gain_reduce,
    bias_reduce,
    conv_group,
    gain_group,
    bias_group,
    conv_expand,
    gain_expand,
    bias_expand,
    out_grad,
):
    n, side, _, C = image_in.shape
    W = conv_reduce.shape[1]
    cg = conv_group.shape[3]
    rows = side * side * n
    dims = (n, side, C, W, grp, dp, cg)
    devices = grp * dp
    half = W // 2
    taps_rows = 9 * conv_group.shape[2]
    par1 = jnp.stack([gain_reduce, bias_reduce]).astype(F32)
    par3 = jnp.stack([gain_expand, bias_expand]).astype(F32)
    packed = jnp.concatenate(
        [
            conv_group.reshape(taps_rows, cg),
            gain_group.reshape(1, cg),
            bias_group.reshape(1, cg),
            jnp.zeros((14, cg), BF),
        ]
    )
    x = pixels_first(image_in)
    upstream = pixels_first(out_grad)
    any_spec = pl.BlockSpec(memory_space=pl.ANY)
    vmem = pl.BlockSpec(memory_space=pltpu.VMEM)
    smem = pl.BlockSpec(memory_space=pltpu.SMEM)
    sds = jax.ShapeDtypeStruct
    dma = pltpu.SemaphoreType.DMA
    blocks = W // CB
    span = rows + 2 * side * n
    parts = C // 512
    tap_units = -(-taps_rows * blocks // (16 * devices))
    stages = 2 * sum(len(bits) for bits in index_bits(grp, dp))

    def params(which):
        return pltpu.CompilerParams(
            collective_id=which, has_side_effects=True, vmem_limit_bytes=VMEM_LIMIT
        )

    red, mixed, p1, p2, wgall = pl.pallas_call(
        functools.partial(ka_kernel, dims),
        name="forward_a",
        out_shape=(
            sds((rows, W), F32),
            sds((rows, W), F32),
            sds((8, W), F32),
            sds((8, W), F32),
            sds((grp, taps_rows + 16, cg), BF),
        ),
        in_specs=[any_spec, any_spec, any_spec, vmem, smem],
        out_specs=(any_spec, any_spec, vmem, vmem, any_spec),
        scratch_shapes=[
            pltpu.VMEM((rows, C), BF),
            pltpu.VMEM((C, W), BF),
            pltpu.VMEM((rows, W), F32),
            pltpu.VMEM((rows, W), F32),
            pltpu.VMEM((grp, taps_rows + 16, cg), BF),
            pltpu.VMEM((blocks, 6 * CB, 2 * CB), BF),
            pltpu.VMEM((span, 3 * CB), BF),
            pltpu.VMEM((devices, 1, 128), F32),
            pltpu.VMEM((2, devices, 2, half), F32),
            pltpu.VMEM((2, devices, 2, half), F32),
            dma((5,)),
            dma((4,)),
            dma((2, grp - 1)),
            dma((2,)),
            dma((2, 2)),
            dma((2, 2)),
        ],
        compiler_params=params(0),
    )(x, conv_reduce, packed, par1, slot_mask)

    block_out, pre, ein, h2, sums3 = pl.pallas_call(
        functools.partial(kb_kernel, dims),
        name="middle_b",
        out_shape=(
            sds((rows, C), BF),
            sds((rows, C), F32),
            sds((rows, C), BF),
            sds((rows, W), BF),
            sds((2, C), F32),
        ),
        in_specs=[any_spec, vmem, any_spec, any_spec, any_spec, vmem, smem],
        out_specs=(any_spec, any_spec, any_spec, any_spec, vmem),
        scratch_shapes=[
            pltpu.VMEM((rows, W), F32),
            pltpu.VMEM((W, C), BF),
            pltpu.VMEM((rows, W), BF),
            pltpu.VMEM((rows, C), F32),
            pltpu.VMEM((rows, C), BF),
            pltpu.VMEM((rows, C), BF),
            pltpu.VMEM((rows, C), BF),
            pltpu.VMEM((8, C), F32),
            pltpu.VMEM((devices, 1, 128), F32),
            pltpu.VMEM((parts, devices, 2, 512), F32),
            pltpu.VMEM((parts, devices, 2, 512), F32),
            dma((10,)),
            dma((3 + parts,)),
            dma((2,)),
            dma((2, parts)),
            dma((2, parts)),
        ],
        compiler_params=params(1),
    )(mixed, p2, conv_expand, x, upstream, par3, slot_mask)

    flat = W * C // 128
    image_grad, rwg_sum, ewg_sum, gwg_sum, sums1, sums2 = pl.pallas_call(
        functools.partial(kc_kernel, dims),
        name="backward_c",
        out_shape=(
            sds((rows, C), BF),
            sds((flat, 128), BF),
            sds((flat, 128), BF),
            sds((tap_units * 16 * devices, 128), BF),
            sds((2, W), F32),
            sds((2, W), F32),
        ),
        in_specs=[any_spec] * 5 + [vmem] * 3 + [any_spec] * 3 + [smem],
        out_specs=(any_spec, any_spec, any_spec, any_spec, vmem, vmem),
        scratch_shapes=[
            pltpu.VMEM((rows, W), BF),
            pltpu.VMEM((rows, W), BF),
            pltpu.VMEM((rows, W), F32),
            pltpu.VMEM((rows, W), F32),
            pltpu.VMEM((rows, C), BF),
            pltpu.VMEM((C // W, W, W), BF),
            pltpu.VMEM((2, rows // 2, 512), F32),
            pltpu.VMEM((flat, 128), BF),
            pltpu.VMEM((flat, 128), BF),
            pltpu.VMEM((flat, 128), BF),
            pltpu.VMEM((flat, 128), BF),
            pltpu.VMEM((tap_units * 16 * devices, 128), BF),
            pltpu.VMEM((tap_units * 16 * devices, 128), BF),
            pltpu.VMEM((2 * CB, 6 * CB), BF),
            pltpu.VMEM((span, 3 * CB), BF),
            pltpu.VMEM((span, CB), BF),
            pltpu.VMEM((8, W), F32),
            pltpu.VMEM((2, devices, 2, half), F32),
            pltpu.VMEM((2, devices, 2, half), F32),
            dma((16,)),
            dma((2,)),
            dma((parts,)),
            dma((2, 2)),
            dma((2, 2)),
            dma((2, 2, 3, stages)),
            dma((2, 2, 3, stages)),
            dma((2, 3, stages)),
            dma((5, 3)),
        ],
        compiler_params=params(2),
    )(mixed, red, ein, h2, conv_expand, p1, p2, wgall, x, conv_reduce, pre, slot_mask)

    shard = cg // CB
    gwg_sum = gwg_sum[: taps_rows * blocks].reshape(blocks, taps_rows, CB)
    gwg_sum = lax.dynamic_slice_in_dim(gwg_sum, lax.axis_index("grp") * shard, shard, 0)
    group_wgrad = columns_last(gwg_sum)
    own = lax.dynamic_slice_in_dim(sums2, lax.axis_index("grp") * cg, cg, 1)
    return (
        images_first(block_out, n, side),
        images_first(image_grad, n, side),
        columns_last(rwg_sum.reshape(W // 128, C, 128)),
        sums1[0],
        sums1[1],
        group_wgrad.reshape(conv_group.shape),
        own[0],
        own[1],
        columns_last(ewg_sum.reshape(C // 128, W, 128)),
        sums3[0],
        sums3[1],
    )


def solution(mesh):
    placed = (
        P(("grp", "dp"), None, None, None),
        P(("grp", "dp")),
        P(),
        P(),
        P(),
        P(None, None, None, "grp"),
        P("grp"),
        P("grp"),
        P(),
        P(),
        P(),
        P(("grp", "dp"), None, None, None),
    )
    return jax.shard_map(
        functools.partial(per_device, mesh.shape["grp"], mesh.shape["dp"]),
        mesh=mesh,
        in_specs=placed,
        out_specs=(
            P(("grp", "dp"), None, None, None),
            P(("grp", "dp"), None, None, None),
            P(),
            P(),
            P(),
            P(None, None, None, "grp"),
            P("grp"),
            P("grp"),
            P(),
            P(),
            P(),
        ),
        check_vma=False,
    )
```

```python
import functools

import jax
import jax.numpy as jnp
from jax import lax
from jax.experimental import pallas as pl
from jax.experimental.pallas import tpu as pltpu
from jax.sharding import PartitionSpec as P

EPS = 1e-05
BF = jnp.bfloat16
F32 = jnp.float32
MESH = pl.DeviceIdType.MESH
CB = 128
VMEM_LIMIT = 61952 * 1024


def aligned(index, size):
    return pl.ds(pl.multiple_of(index * size, size), size)


def sigmoid(values):
    return 0.5 * jnp.tanh(0.5 * values) + 0.5


def fold(values, images):
    rows, cols = values.shape
    return jnp.sum(values.reshape(rows // images, images, cols), axis=0)


def down(values):
    return jnp.sum(values, axis=0, keepdims=True)


def spread_rows(values, row):
    rows, cols = values.shape
    images = row.shape[0]
    return (values.reshape(rows // images, images, cols) * wide(row, cols)[None]).reshape(rows, cols)


class Links:
    def __init__(self, grp, dp):
        self.grp, self.dp = grp, dp
        self.count = grp * dp
        self.g, self.d = lax.axis_index("grp"), lax.axis_index("dp")
        self.me = self.g * dp + self.d

    def peer(self, step):
        target = lax.rem(self.me + step, self.count)
        return (target // self.dp, lax.rem(target, self.dp))

    def greet(self):
        barrier = pltpu.get_barrier_semaphore()

        @pl.loop(1, self.count)
        def _(step):
            pl.semaphore_signal(barrier, inc=1, device_id=self.peer(step), device_id_type=MESH)

    def greeted(self):
        pl.semaphore_wait(pltpu.get_barrier_semaphore(), self.count - 1)

    def send(self, buf, send_sem, recv_sem):
        @pl.loop(1, self.count)
        def _(step):
            pltpu.make_async_remote_copy(
                src_ref=buf.at[self.me],
                dst_ref=buf.at[self.me],
                send_sem=send_sem,
                recv_sem=recv_sem,
                device_id=self.peer(step),
                device_id_type=MESH,
            ).start()

    def wait(self, buf, send_sem, recv_sem):
        others = buf.at[pl.ds(0, self.count - 1)]
        copy = pltpu.make_async_remote_copy(
            src_ref=others,
            dst_ref=others,
            send_sem=send_sem,
            recv_sem=recv_sem,
            device_id=self.peer(1),
            device_id_type=MESH,
        )
        copy.wait_recv()
        copy.wait_send()


def index_bits(grp, dp):
    ones = lambda count: [1 << k for k in range(count.bit_length() - 1)]
    g_bits = [("grp", w) for w in ones(grp)]
    d_bits = [("dp", w) for w in ones(dp)]
    low = len(d_bits) // 2
    return g_bits[:1], g_bits[1:], d_bits[:low], d_bits[low:]


class Reduction:
    def __init__(self, links, buf, recv, out, sems, own_sems):
        self.links, self.buf, self.recv, self.out = links, buf, recv, out
        self.sems, self.own_sems = sems, own_sems
        core, y, x, z = index_bits(links.grp, links.dp)
        orders = (core + x + y + z, core + y + x + z, core + z + x + y)
        unit = 16 * links.count
        units = buf.shape[0] // unit
        last = units // 4
        sizes = ((units - last + 1) // 2, (units - last) // 2, last)
        self.parts = []
        start = 0
        for order, size in zip(orders, sizes):
            if size:
                self.parts.append(dict(start=start, size=size * unit, lo=start, order=order))
            start += size * unit
        self.bits = len(orders[0])
        self.stage = 0
        self.started = False

    def place(self, bit):
        axis, weight = bit
        at = self.links.g if axis == "grp" else self.links.d
        value = lax.rem(at // weight, 2)
        other = at + weight * (1 - 2 * value)
        return value, (other, self.links.d) if axis == "grp" else (self.links.g, other)

    def copy(self, index, part):
        rows = lambda lo, size: pl.ds(pl.multiple_of(lo, 16), size)
        halving = self.stage < self.bits
        bit = part["order"][self.stage if halving else 2 * self.bits - 1 - self.stage]
        value, device = self.place(bit)
        if halving:
            half = part["size"] // 2
            src = self.buf.at[rows(part["lo"] + (1 - value) * half, half)]
            dst = self.recv.at[rows(part["start"], half)]
        else:
            here = self.buf if self.stage == self.bits else self.out
            src = here.at[rows(part["lo"], part["size"])]
            dst = self.out.at[rows(part["lo"], part["size"])]
        return value, pltpu.make_async_remote_copy(
            src_ref=src,
            dst_ref=dst,
            send_sem=self.sems.at[0, index, self.stage],
            recv_sem=self.sems.at[1, index, self.stage],
            device_id=device,
            device_id_type=MESH,
        )

    def start(self, now=0.0):
        self.started = True
        for index, part in enumerate(self.parts):
            self.copy(index, part)[1].start()
        self.ready = now + self.estimate()

    def estimate(self):
        halving = self.stage < self.bits
        longest = 0.0
        for part in self.parts:
            kilobytes = (part["size"] // 2 if halving else part["size"]) * 0.256
            near = self.stage in (0, 2 * self.bits - 1)
            longest = max(longest, 1.5 + kilobytes / 400 if near else 3.5 + kilobytes / 25)
        return longest

    def advance(self, now=0.0):
        for index, part in enumerate(self.parts):
            value, copy = self.copy(index, part)
            copy.wait()
            if self.stage < self.bits:
                half = part["size"] // 2
                keep, base = part["lo"] + value * half, part["start"]
                chunk = max(c for c in range(16, 513, 16) if half % c == 0)

                @pl.loop(0, half // chunk)
                def _(k):
                    at = pl.ds(pl.multiple_of(keep + k * chunk, 16), chunk)
                    more = self.recv[pl.ds(pl.multiple_of(base + k * chunk, 16), chunk), :]
                    self.buf[at, :] = (self.buf[at, :].astype(F32) + more.astype(F32)).astype(BF)

                part.update(lo=keep, size=half, start=base + half)
                if self.stage == self.bits - 1:
                    at = pl.ds(pl.multiple_of(keep, 16), half)
                    part["own"] = pltpu.make_async_copy(
                        self.buf.at[at], self.out.at[at], self.own_sems.at[index]
                    )
                    part["own"].start()
            else:
                if self.stage == self.bits:
                    part["own"].wait()
                part.update(lo=part["lo"] - value * part["size"], size=2 * part["size"])
            if self.stage + 1 < 2 * self.bits:
                self.stage += 1
                self.copy(index, part)[1].start()
                self.stage -= 1
        self.stage += 1
        self.ready = now + self.estimate()

    def busy(self):
        return self.started and self.stage < 2 * self.bits


class Clock:
    def __init__(self, reductions):
        self.now, self.reductions = 0.0, reductions

    def spend(self, microseconds):
        self.now += microseconds
        for each in self.reductions:
            if each.busy() and each.ready <= self.now:
                each.advance(self.now)

    def finish(self):
        while any(each.busy() for each in self.reductions):
            for each in self.reductions:
                if each.busy():
                    each.advance(self.now)


def wide(row, cols):
    return jnp.concatenate([row] * (cols // 128), axis=-1)


def row_weights(mask_ref, images):
    at = lax.broadcasted_iota(jnp.int32, (images, 128), 0)
    column = jnp.zeros((images, 128), F32)
    count = jnp.float32(0.0)
    for i in range(images):
        value = mask_ref[i].astype(F32)
        column = jnp.where(at == i, value, column)
        count = count + value
    return column, count


def merge_stats(buf, counts, cols):
    each = wide(counts, cols)
    total = jnp.sum(each, axis=0)
    parts = buf[...]
    means, squares = parts[:, 0:1], parts[:, 1:2]
    average = jnp.sum(each * means, axis=0) / total
    gap = means - average
    spread = jnp.sum(squares + each * gap * gap, axis=0) / total
    return average, lax.rsqrt(spread + EPS)


def dense_taps(shard):
    group = 32
    row = lax.broadcasted_iota(jnp.int32, (CB, CB), 0) // group
    col = lax.broadcasted_iota(jnp.int32, (CB, CB), 1) // group
    keep = row == col
    zero = jnp.zeros((CB, CB), BF)

    def block(row_tap, col_tap, turned=False):
        start = (row_tap * 3 + col_tap) * group
        tile = shard(start, group).astype(F32)
        full = jnp.concatenate([tile] * (CB // group), axis=0)
        full = jnp.where(keep, full, 0.0)
        return (full.T if turned else full).astype(BF)

    return block, zero


def shifted(values, images):
    edge = jnp.zeros((images, values.shape[1]), F32)
    return (
        jnp.concatenate([edge, values[:-images]], axis=0),
        jnp.concatenate([values[images:], edge], axis=0),
    )


def local_stats(field, cols, mean_of, rows, chunk, images, row, inverse, width):
    mean = down(mean_of * wide(row, width)) * wide(inverse, width)

    def body(k, acc):
        gap = field[aligned(k, chunk), cols] - mean
        return acc + fold(gap * gap, images)

    squares = lax.fori_loop(0, rows // chunk, body, jnp.zeros((images, width), F32))
    return mean, down(squares * wide(row, width))


def ka_kernel(
    dims,
    x_hbm,
    wr_hbm,
    wg_hbm,
    par_ref,
    mask_ref,
    red_hbm,
    mixed_hbm,
    p1_ref,
    p2_ref,
    back_hbm,
    xv,
    wr,
    red,
    mixed,
    wgall,
    taps,
    back,
    hbuf,
    cnt,
    ex1,
    ex2,
    load_sem,
    store_sem,
    gather_sem,
    cnt_sem,
    ex1_sem,
    ex2_sem,
):
    n, side, C, W, grp, dp, cg = dims
    rows = side * side * n
    line = side * n
    half = W // 2
    tile = rows // 2
    links = Links(grp, dp)
    links.greet()
    w_loads = [
        pltpu.make_async_copy(
            wr_hbm.at[:, pl.ds(h * half, half)], wr.at[:, pl.ds(h * half, half)], load_sem.at[h]
        )
        for h in range(2)
    ]
    x_loads = [
        pltpu.make_async_copy(
            x_hbm.at[pl.ds(h * tile, tile), :], xv.at[pl.ds(h * tile, tile), :], load_sem.at[2 + h]
        )
        for h in range(2)
    ]
    w_loads[0].start()
    x_loads[0].start()
    x_loads[1].start()
    w_loads[1].start()
    own = pltpu.make_async_copy(wg_hbm, wgall.at[links.g], load_sem.at[4])
    own.start()

    row, valid = row_weights(mask_ref, n)
    local = jnp.full((1, 128), 1.0, F32) * (valid * float(side * side))
    cnt[links.me] = local
    inverse = 1.0 / jnp.maximum(local, 1.0)
    hbuf[...] = jnp.zeros(hbuf.shape, BF)
    links.greeted()
    links.send(cnt, cnt_sem.at[0], cnt_sem.at[1])
    gathers = []
    for k in range(1, grp):
        copy = pltpu.make_async_remote_copy(
            src_ref=wg_hbm,
            dst_ref=wgall.at[links.g],
            send_sem=gather_sem.at[0, k - 1],
            recv_sem=gather_sem.at[1, k - 1],
            device_id=(lax.rem(links.g + k, grp), links.d),
            device_id_type=MESH,
        )
        copy.start()
        gathers.append(copy)

    for h in range(2):
        w_loads[h].wait()
        cols = pl.ds(h * half, half)
        total = jnp.zeros((n, half), F32)
        for t in range(2):
            if h == 0:
                x_loads[t].wait()
            at = pl.ds(t * tile, tile)
            out = jnp.dot(xv[at, :], wr[:, cols], preferred_element_type=F32)
            red[at, cols] = out
            total += fold(out, n)
        mean, squares = local_stats(red, cols, total, rows, line, n, row, inverse, half)
        ex1[h, links.me, 0:1, :] = mean
        ex1[h, links.me, 1:2, :] = squares
        if h == 0:
            links.wait(cnt, cnt_sem.at[0], cnt_sem.at[1])
        links.send(ex1.at[h], ex1_sem.at[0, h], ex1_sem.at[1, h])
    red_store = pltpu.make_async_copy(red, red_hbm, store_sem.at[0])
    red_store.start()

    own.wait()
    for copy in gathers:
        copy.wait()
    blocks = W // CB
    per_shard = cg // CB

    @pl.loop(0, blocks)
    def _(b):
        shard_at, lane = b // per_shard, aligned(lax.rem(b, per_shard), CB)
        block, zero = dense_taps(lambda start, size: wgall[shard_at, pl.ds(start, size), lane])
        for dx in range(3):
            taps[b, pl.ds(dx * CB, CB), 0:CB] = block(0, dx)
            taps[b, pl.ds(dx * CB, CB), CB : 2 * CB] = zero
            taps[b, pl.ds((3 + dx) * CB, CB), 0:CB] = block(1, dx)
            taps[b, pl.ds((3 + dx) * CB, CB), CB : 2 * CB] = block(2, dx)
            back[b, pl.ds(dx * CB, CB), 0:CB] = block(2, 2 - dx, True)
            back[b, pl.ds(dx * CB, CB), CB : 2 * CB] = zero
            back[b, pl.ds((3 + dx) * CB, CB), 0:CB] = block(1, 2 - dx, True)
            back[b, pl.ds((3 + dx) * CB, CB), CB : 2 * CB] = block(0, 2 - dx, True)

    store_back = pltpu.make_async_copy(back, back_hbm, store_sem.at[1])
    store_back.start()

    for h in range(2):
        links.wait(ex1.at[h], ex1_sem.at[0, h], ex1_sem.at[1, h])
        cols = pl.ds(h * half, half)
        average, scale = merge_stats(ex1.at[h], cnt[...], half)
        p1_ref[0:1, cols] = average
        p1_ref[1:2, cols] = scale

        @pl.loop(h * blocks // 2, (h + 1) * blocks // 2)
        def _(b):
            lanes = aligned(b, CB)
            mean, rstd = p1_ref[0:1, lanes], p1_ref[1:2, lanes]
            gain, shift = par_ref[0:1, lanes], par_ref[1:2, lanes]

            @pl.loop(0, side)
            def _(r):
                act = (red[aligned(r, line), lanes] - mean) * rstd * gain + shift
                hidden = act * sigmoid(act)
                left, right = shifted(hidden, n)
                to = aligned(r + 1, line)
                hbuf[to, 0:CB] = left.astype(BF)
                hbuf[to, CB : 2 * CB] = hidden.astype(BF)
                hbuf[to, 2 * CB : 3 * CB] = right.astype(BF)

            lhs = jnp.concatenate([hbuf[0 : rows + line, :], hbuf[line : rows + 2 * line, :]], axis=1)
            out = jnp.dot(lhs, taps[b], preferred_element_type=F32)
            field = out[0:rows, 0:CB] + out[line : line + rows, CB:]
            mixed[:, lanes] = field
            mean, squares = local_stats(
                mixed, lanes, fold(field, n), rows, line, n, row, inverse, CB
            )
            inner = aligned(lax.rem(b, blocks // 2), CB)
            ex2[h, links.me, 0:1, inner] = mean
            ex2[h, links.me, 1:2, inner] = squares

        links.send(ex2.at[h], ex2_sem.at[0, h], ex2_sem.at[1, h])
        pltpu.make_async_copy(mixed.at[:, cols], mixed_hbm.at[:, cols], store_sem.at[2 + h]).start()

    count = jnp.sum(wide(cnt[...], W), axis=0)
    p1_ref[2:3, :] = count
    p2_ref[2:3, :] = count
    extra = jnp.concatenate(
        [wgall[k, pl.ds(9 * 32, 16), :].astype(F32) for k in range(grp)], axis=1
    )
    p2_ref[3:5, :] = extra[0:2]
    p1_ref[3:5, :] = par_ref[0:2, :]
    for h in range(2):
        links.wait(ex2.at[h], ex2_sem.at[0, h], ex2_sem.at[1, h])
        cols = pl.ds(h * half, half)
        average, scale = merge_stats(ex2.at[h], cnt[...], half)
        p2_ref[0:1, cols] = average
        p2_ref[1:2, cols] = scale
    red_store.wait()
    store_back.wait()
    for h in range(2):
        cols = pl.ds(h * half, half)
        pltpu.make_async_copy(mixed.at[:, cols], mixed_hbm.at[:, cols], store_sem.at[2 + h]).wait()


def kb_kernel(
    dims,
    mixed_hbm,
    p2_ref,
    we_hbm,
    x_hbm,
    dout_hbm,
    par_ref,
    mask_ref,
    out_hbm,
    pre_hbm,
    ein_hbm,
    h2_hbm,
    sums3_ref,
    mixed,
    we,
    h2,
    expd,
    xe,
    dout,
    n3,
    stat3,
    cnt,
    ex3,
    ex4,
    load_sem,
    store_sem,
    cnt_sem,
    ex3_sem,
    ex4_sem,
):
    n, side, C, W, grp, dp, cg = dims
    rows = side * side * n
    line = side * n
    tile = rows // 2
    links = Links(grp, dp)
    links.greet()
    part_cols = 512
    parts = C // part_cols
    pieces = 7
    piece = rows // pieces
    m_loads = [
        pltpu.make_async_copy(
            mixed_hbm.at[pl.ds(k * piece, piece), :],
            mixed.at[pl.ds(k * piece, piece), :],
            load_sem.at[k],
        )
        for k in range(pieces)
    ]
    for copy in m_loads:
        copy.start()
    we_load = pltpu.make_async_copy(we_hbm, we, load_sem.at[pieces])
    we_load.start()
    x_load = pltpu.make_async_copy(x_hbm, xe, load_sem.at[pieces + 1])
    x_load.start()
    d_load = pltpu.make_async_copy(dout_hbm, dout, load_sem.at[pieces + 2])
    d_load.start()
    row, valid = row_weights(mask_ref, n)
    local = jnp.full((1, 128), 1.0, F32) * (valid * float(side * side))
    cnt[links.me] = local
    inverse = 1.0 / jnp.maximum(local, 1.0)
    links.greeted()
    links.send(cnt, cnt_sem.at[0], cnt_sem.at[1])

    step = 256
    lines = rows // line
    for k in range(pieces):
        m_loads[k].wait()

        @pl.loop(k * lines // pieces, (k + 1) * lines // pieces)
        def _(r):
            at = aligned(r, line)
            for q in range(W // step):
                lanes = pl.ds(q * step, step)
                normed = (mixed[at, lanes] - p2_ref[0:1, lanes]) * p2_ref[1:2, lanes]
                act = normed * p2_ref[3:4, lanes] + p2_ref[4:5, lanes]
                h2[at, lanes] = (act * sigmoid(act)).astype(BF)

    h2_store = pltpu.make_async_copy(h2, h2_hbm, store_sem.at[2])
    h2_store.start()

    we_load.wait()
    links.wait(cnt, cnt_sem.at[0], cnt_sem.at[1])
    for part in range(parts):
        cols = pl.ds(part * part_cols, part_cols)
        total = jnp.zeros((n, part_cols), F32)
        for t in range(2):
            at = pl.ds(t * tile, tile)
            out = jnp.dot(h2[at, :], we[:, cols], preferred_element_type=F32)
            expd[at, cols] = out
            total += fold(out, n)
        mean, squares = local_stats(expd, cols, total, rows, line, n, row, inverse, part_cols)
        ex3[part, links.me, 0:1, :] = mean
        ex3[part, links.me, 1:2, :] = squares
        links.send(ex3.at[part], ex3_sem.at[0, part], ex3_sem.at[1, part])

    x_load.wait()
    d_load.wait()
    step = 128
    for part in range(parts):
        cols = pl.ds(part * part_cols, part_cols)
        links.wait(ex3.at[part], ex3_sem.at[0, part], ex3_sem.at[1, part])
        average, scale = merge_stats(ex3.at[part], cnt[...], part_cols)
        stat3[0:1, cols] = average
        stat3[1:2, cols] = scale

        @pl.loop(0, part_cols // step)
        def _(q):
            lanes = pl.ds(pl.multiple_of(part * part_cols + q * step, step), step)
            mean, rstd = stat3[0:1, lanes], stat3[1:2, lanes]
            gain, shift = par_ref[0:1, lanes], par_ref[1:2, lanes]

            def body(r, sums):
                at = aligned(r, line)
                normed = (expd[at, lanes] - mean) * rstd
                summed = normed * gain + shift + xe[at, lanes].astype(F32)
                sig = sigmoid(summed)
                silu = summed * sig
                grad = spread_rows(dout[at, lanes].astype(F32), row) * (sig + silu * (1.0 - sig))
                dout[at, lanes] = spread_rows(silu, row).astype(BF)
                expd[at, lanes] = grad
                n3[at, lanes] = normed.astype(BF)
                return sums[0] + fold(grad * normed, n), sums[1] + fold(grad, n)

            zeros = jnp.zeros((n, step), F32)
            gain_sum, shift_sum = lax.fori_loop(0, lines, body, (zeros, zeros))
            inner = aligned(q, step)
            ex4[part, links.me, 0:1, inner] = down(gain_sum)
            ex4[part, links.me, 1:2, inner] = down(shift_sum)

        links.send(ex4.at[part], ex4_sem.at[0, part], ex4_sem.at[1, part])
    out_store = pltpu.make_async_copy(dout, out_hbm, store_sem.at[0])
    out_store.start()
    pre_store = pltpu.make_async_copy(expd, pre_hbm, store_sem.at[1])
    pre_store.start()

    total = jnp.sum(wide(cnt[...], part_cols), axis=0)
    ein_stores = []
    for part in range(parts):
        cols = pl.ds(part * part_cols, part_cols)
        links.wait(ex4.at[part], ex4_sem.at[0, part], ex4_sem.at[1, part])
        sums = jnp.sum(ex4[part], axis=0)
        sums3_ref[0:2, cols] = sums
        stat3[2:3, cols] = sums[0:1] / total
        stat3[3:4, cols] = sums[1:2] / total
        stat3[4:5, cols] = par_ref[0:1, cols] * stat3[1:2, cols]

        @pl.loop(0, lines)
        def _(r):
            at = aligned(r, line)
            for q in range(part_cols // step):
                lanes = pl.ds(part * part_cols + q * step, step)
                off = stat3[3:4, lanes] + n3[at, lanes].astype(F32) * stat3[2:3, lanes]
                value = stat3[4:5, lanes] * (expd[at, lanes] - spread_rows(off, row))
                xe[at, lanes] = value.astype(BF)
        store = pltpu.make_async_copy(xe.at[:, cols], ein_hbm.at[:, cols], store_sem.at[3 + part])
        store.start()
        ein_stores.append(store)
    h2_store.wait()
    out_store.wait()
    pre_store.wait()
    for store in ein_stores:
        store.wait()


def kc_kernel(
    dims,
    mixed_hbm,
    red_hbm,
    ein_hbm,
    h2_hbm,
    we_hbm,
    p1_ref,
    p2_ref,
    back_hbm,
    x_hbm,
    wr_hbm,
    pre_hbm,
    mask_ref,
    ig_hbm,
    rwg_hbm,
    ewg_hbm,
    gwg_hbm,
    sums1_ref,
    sums2_ref,
    h2,
    h2g,
    mixed,
    red,
    xv,
    weight,
    pre,
    ewg,
    ewg_in,
    rwg,
    rwg_in,
    gwg,
    gwg_in,
    taps,
    dbuf,
    hbuf,
    coef,
    ex5,
    ex6,
    load_sem,
    pre_sem,
    taps_sem,
    store_sem,
    ex5_sem,
    ex6_sem,
    ewg_sem,
    rwg_sem,
    gwg_sem,
    own_sem,
):
    n, side, C, W, grp, dp, cg = dims
    rows = side * side * n
    line = side * n
    half = W // 2
    tile = rows // 2
    blocks = W // CB
    part_cols = 512
    parts = C // part_cols
    group = 32
    links = Links(grp, dp)
    links.greet()

    used = []

    def load(src, dst):
        copy = pltpu.make_async_copy(src, dst, load_sem.at[len(used)])
        used.append(copy)
        copy.start()
        return copy

    column = lambda k, width: pl.ds(k * width, width)
    h2_load = load(h2_hbm, h2)
    ein_loads = [
        load(ein_hbm.at[:, column(k, part_cols)], xv.at[:, column(k, part_cols)])
        for k in range(parts)
    ]
    we_loads = [load(we_hbm.at[:, column(k, W)], weight.at[k]) for k in range(C // W)]
    mixed_loads = [
        load(mixed_hbm.at[:, column(h, half)], mixed.at[:, column(h, half)]) for h in range(2)
    ]
    red_loads = [load(red_hbm.at[:, column(h, half)], red.at[:, column(h, half)]) for h in range(2)]
    pre_loads = [
        pltpu.make_async_copy(
            pre_hbm.at[pl.ds(t * tile, tile), column(part, part_cols)], pre.at[t], pre_sem.at[t]
        )
        for part in range(parts)
        for t in range(2)
    ]
    taps_loads = [
        pltpu.make_async_copy(back_hbm.at[b], taps.at[b % 2], taps_sem.at[b % 2])
        for b in range(blocks)
    ]
    taps_loads[0].start()
    taps_loads[1].start()
    pre_loads[0].start()
    pre_loads[1].start()
    half_rows = half // 128 * C
    pick = lambda h, refs: [ref.at[pl.ds(h * half_rows, half_rows)] for ref in refs]
    expand_sums = [
        Reduction(links, *pick(h, (ewg, ewg_in, ewg_hbm)), ewg_sem.at[h], own_sem.at[h])
        for h in range(2)
    ]
    reduce_sums = [
        Reduction(links, *pick(h, (rwg, rwg_in, rwg_hbm)), rwg_sem.at[h], own_sem.at[2 + h])
        for h in range(2)
    ]
    group_sum = Reduction(links, gwg, gwg_in, gwg_hbm, gwg_sem, own_sem.at[4])
    clock = Clock(expand_sums + reduce_sums + [group_sum])
    gwg[...] = jnp.zeros(gwg.shape, BF)
    row, valid = row_weights(mask_ref, n)
    dbuf[...] = jnp.zeros(dbuf.shape, BF)
    hbuf[...] = jnp.zeros(hbuf.shape, BF)
    total = p2_ref[2:3, 0:half]
    keep = (
        lax.broadcasted_iota(jnp.int32, (CB, CB), 0) // group
        == lax.broadcasted_iota(jnp.int32, (CB, CB), 1) // group
    )
    transposed = (((0,), (0,)), ((), ()))
    rowwise = (((1,), (1,)), ((), ()))

    h2_load.wait()
    for part in range(parts):
        ein_loads[part].wait()
        out = lax.dot_general(
            h2[...], xv[:, column(part, part_cols)], transposed, preferred_element_type=F32
        )
        for q in range(part_cols // 128):
            at = pl.ds((part * (part_cols // 128) + q) * W, W)
            ewg[at, :] = out[:, q * 128 : (q + 1) * 128].astype(BF)
        if part == 0:
            links.greeted()
        clock.spend(2.3)
        if part % 2:
            expand_sums[part // 2].start(clock.now)

    for copy in we_loads:
        copy.wait()
    step = CB
    for h in range(2):
        cols = column(h, half)
        both = jnp.concatenate([weight[k, cols, :] for k in range(C // W)], axis=1)
        for t in range(2):
            at = pl.ds(t * tile, tile)
            h2g[at, cols] = lax.dot_general(
                xv[at, :], both, rowwise, preferred_element_type=F32
            ).astype(BF)
            clock.spend(2.4)
        mixed_loads[h].wait()

        @pl.loop(0, half // step)
        def _(q):
            lanes = pl.ds(pl.multiple_of(h * half + q * step, step), step)
            mean, rstd = p2_ref[0:1, lanes], p2_ref[1:2, lanes]
            gain, shift = p2_ref[3:4, lanes], p2_ref[4:5, lanes]

            def body(r, sums):
                at = aligned(r, line)
                normed = (mixed[at, lanes] - mean) * rstd
                act = normed * gain + shift
                sig = sigmoid(act)
                grad = h2g[at, lanes].astype(F32) * (sig + act * sig * (1.0 - sig))
                return sums[0] + fold(grad * normed, n), sums[1] + fold(grad, n)

            zeros = jnp.zeros((n, step), F32)
            gain_sum, shift_sum = lax.fori_loop(0, side, body, (zeros, zeros))
            inner = aligned(q, step)
            ex5[h, links.me, 0:1, inner] = down(gain_sum)
            ex5[h, links.me, 1:2, inner] = down(shift_sum)

        links.send(ex5.at[h], ex5_sem.at[0, h], ex5_sem.at[1, h])
        clock.spend(2.0)
    x_load = load(x_hbm, xv)
    wr_loads = [load(wr_hbm.at[column(k, W), :], weight.at[k]) for k in range(C // W)]

    def second_sums(h):
        cols = column(h, half)
        links.wait(ex5.at[h], ex5_sem.at[0, h], ex5_sem.at[1, h])
        sums = jnp.sum(ex5[h], axis=0)
        sums2_ref[0:2, cols] = sums
        coef[0:1, cols] = sums[0:1] / total
        coef[1:2, cols] = sums[1:2] / total
        coef[2:3, cols] = p2_ref[3:4, cols] * p2_ref[1:2, cols]
        red_loads[h].wait()

    def conv_block(h, b):
        lanes = pl.ds(b * CB, CB)

        @pl.loop(0, side)
        def _(r):
            at = aligned(r, line)
            normed = (mixed[at, lanes] - p2_ref[0:1, lanes]) * p2_ref[1:2, lanes]
            act = normed * p2_ref[3:4, lanes] + p2_ref[4:5, lanes]
            sig = sigmoid(act)
            grad = h2g[at, lanes].astype(F32) * (sig + act * sig * (1.0 - sig))
            off = coef[1:2, lanes] + normed * coef[0:1, lanes]
            grad = coef[2:3, lanes] * (grad - spread_rows(off, row))
            left, right = shifted(grad, n)
            to = aligned(r + 1, line)
            dbuf[to, 0:CB] = left.astype(BF)
            dbuf[to, CB : 2 * CB] = grad.astype(BF)
            dbuf[to, 2 * CB : 3 * CB] = right.astype(BF)

        lhs = jnp.concatenate([dbuf[0 : rows + line, :], dbuf[line : rows + 2 * line, :]], axis=1)
        taps_loads[b].wait()
        out = jnp.dot(lhs, taps[b % 2], preferred_element_type=F32)
        mixed[:, lanes] = out[0:rows, 0:CB] + out[line : line + rows, CB:]
        if b + 2 < blocks:
            taps_loads[b + 2].start()
        mean, rstd = p1_ref[0:1, lanes], p1_ref[1:2, lanes]
        gain, shift = p1_ref[3:4, lanes], p1_ref[4:5, lanes]

        def body(r, sums):
            at = aligned(r, line)
            normed = (red[at, lanes] - mean) * rstd
            act = normed * gain + shift
            sig = sigmoid(act)
            silu = act * sig
            hbuf[aligned(r + 1, line), :] = silu.astype(BF)
            grad = mixed[at, lanes].astype(BF).astype(F32) * (sig + silu * (1.0 - sig))
            mixed[at, lanes] = grad
            return sums[0] + fold(grad * normed, n), sums[1] + fold(grad, n)

        zeros = jnp.zeros((n, CB), F32)
        gain_sum, shift_sum = lax.fori_loop(0, side, body, (zeros, zeros))
        inner = pl.ds(b % (blocks // 2) * CB, CB)
        ex6[h, links.me, 0:1, inner] = down(gain_sum)
        ex6[h, links.me, 1:2, inner] = down(shift_sum)
        clock.spend(3.3)

    def conv_wgrad(b):
        span = rows + line
        left = jnp.concatenate([hbuf[0:span, :], hbuf[line : line + span, :]], axis=1)
        right = jnp.concatenate([dbuf[0:span, :], dbuf[line : line + span, :]], axis=1)
        full = lax.dot_general(left, right, transposed, preferred_element_type=F32)
        for dy in range(3):
            left_at, right_at = ((0, 1), (0, 0), (1, 0))[dy]
            for dx in range(3):
                lane_at = (3 * right_at + 2 - dx) * CB
                part = full[left_at * CB : (left_at + 1) * CB, lane_at : lane_at + CB]
                part = jnp.where(keep, part, 0.0)
                picked = functools.reduce(
                    lambda a, b: a + b,
                    [part[k * group : (k + 1) * group] for k in range(CB // group)],
                )
                gwg[pl.ds((b * 9 + dy * 3 + dx) * group, group), :] = picked.astype(BF)
        clock.spend(1.5)

    def reduce_half(h):
        cols = column(h, half)
        links.wait(ex6.at[h], ex6_sem.at[0, h], ex6_sem.at[1, h])
        sums = jnp.sum(ex6[h], axis=0)
        sums1_ref[0:2, cols] = sums
        coef[3:4, cols] = sums[0:1] / total
        coef[4:5, cols] = sums[1:2] / total
        coef[5:6, cols] = p1_ref[3:4, cols] * p1_ref[1:2, cols]

        @pl.loop(0, side)
        def _(r):
            at = aligned(r, line)
            for q in range(half // CB):
                lanes = pl.ds(h * half + q * CB, CB)
                normed = (red[at, lanes] - p1_ref[0:1, lanes]) * p1_ref[1:2, lanes]
                off = coef[4:5, lanes] + normed * coef[3:4, lanes]
                grad = coef[5:6, lanes] * (mixed[at, lanes] - spread_rows(off, row))
                h2g[at, lanes] = grad.astype(BF)

        clock.spend(1.5)
        if h == 0:
            x_load.wait()
        big = C // 2
        for k in range(2):
            out = lax.dot_general(
                xv[:, column(k, big)], h2g[:, cols], transposed, preferred_element_type=F32
            )
            for q in range(half // 128):
                start = (h * (half // 128) + q) * C + k * big
                rwg[pl.ds(start, big), :] = out[:, q * 128 : (q + 1) * 128].astype(BF)
            clock.spend(2.2)
        reduce_sums[h].start(clock.now)

    for b in range(blocks):
        h, first, last = b * 2 // blocks, b % (blocks // 2) == 0, (b + 1) % (blocks // 2) == 0
        if first:
            second_sums(h)
        conv_block(h, b)
        if last:
            links.send(ex6.at[h], ex6_sem.at[0, h], ex6_sem.at[1, h])
        conv_wgrad(b)
        if b == blocks // 2:
            reduce_half(0)
    group_sum.start(clock.now)
    reduce_half(1)

    for copy in wr_loads:
        copy.wait()
    ig_stores = []
    for part in range(parts):
        cols = column(part, part_cols)
        for t in range(2):
            at = pl.ds(t * tile, tile)
            across = part * part_cols
            out = lax.dot_general(
                h2g[at, :],
                weight[across // W, pl.ds(across % W, part_cols), :],
                rowwise,
                preferred_element_type=F32,
            )
            pre_loads[2 * part + t].wait()
            xv[at, cols] = (out + pre[t]).astype(BF)
            if 2 * part + t + 2 < len(pre_loads):
                pre_loads[2 * part + t + 2].start()
            clock.spend(1.2)
        store = pltpu.make_async_copy(xv.at[:, cols], ig_hbm.at[:, cols], store_sem.at[part])
        store.start()
        ig_stores.append(store)
    clock.finish()
    for copy in ig_stores:
        copy.wait()


def pixels_first(field):
    n, side, _, channels = field.shape
    return jnp.transpose(field, (1, 2, 0, 3)).reshape(side * side * n, channels)


def images_first(field, n, side):
    return jnp.transpose(field.reshape(side, side, n, field.shape[1]), (2, 0, 1, 3))


def columns_last(tiles):
    return jnp.transpose(tiles, (1, 0, 2)).reshape(tiles.shape[1], -1).astype(F32)


def wgrads_kernel(reduce_ref, expand_ref, reduce_out, expand_out):
    for source, result in ((reduce_ref, reduce_out), (expand_ref, expand_out)):
        size = result.shape[0]
        for k in range(result.shape[1] // 128):
            result[:, k * 128 : (k + 1) * 128] = source[k * size : (k + 1) * size, :].astype(F32)


def wgrad_results(reduce_flat, expand_flat, C, W):
    steps = W // 128
    block = reduce_flat.shape[0] // steps
    spec = pl.BlockSpec((block, 128), lambda i: (i, 0))
    return pl.pallas_call(
        wgrads_kernel,
        name="wgrad_results",
        grid=(steps,),
        out_shape=(jax.ShapeDtypeStruct((C, W), F32), jax.ShapeDtypeStruct((W, C), F32)),
        in_specs=[spec, spec],
        out_specs=(
            pl.BlockSpec((C, W // steps), lambda i: (0, i)),
            pl.BlockSpec((W, C // steps), lambda i: (0, i)),
        ),
    )(reduce_flat, expand_flat)


def per_device(
    grp,
    dp,
    image_in,
    slot_mask,
    conv_reduce,
    gain_reduce,
    bias_reduce,
    conv_group,
    gain_group,
    bias_group,
    conv_expand,
    gain_expand,
    bias_expand,
    out_grad,
):
    n, side, _, C = image_in.shape
    W = conv_reduce.shape[1]
    cg = conv_group.shape[3]
    rows = side * side * n
    dims = (n, side, C, W, grp, dp, cg)
    devices = grp * dp
    half = W // 2
    taps_rows = 9 * conv_group.shape[2]
    par1 = jnp.stack([gain_reduce, bias_reduce]).astype(F32)
    par3 = jnp.stack([gain_expand, bias_expand]).astype(F32)
    packed = jnp.concatenate(
        [
            conv_group.reshape(taps_rows, cg),
            gain_group.reshape(1, cg),
            bias_group.reshape(1, cg),
            jnp.zeros((14, cg), BF),
        ]
    )
    x = pixels_first(image_in)
    upstream = pixels_first(out_grad)
    any_spec = pl.BlockSpec(memory_space=pl.ANY)
    vmem = pl.BlockSpec(memory_space=pltpu.VMEM)
    smem = pl.BlockSpec(memory_space=pltpu.SMEM)
    sds = jax.ShapeDtypeStruct
    dma = pltpu.SemaphoreType.DMA
    blocks = W // CB
    span = rows + 2 * side * n
    parts = C // 512
    tap_units = -(-taps_rows * blocks // (16 * devices))
    stages = 2 * sum(len(bits) for bits in index_bits(grp, dp))

    def params(which):
        return pltpu.CompilerParams(
            collective_id=which, has_side_effects=True, vmem_limit_bytes=VMEM_LIMIT
        )

    red, mixed, p1, p2, back = pl.pallas_call(
        functools.partial(ka_kernel, dims),
        name="forward_a",
        out_shape=(
            sds((rows, W), F32),
            sds((rows, W), F32),
            sds((8, W), F32),
            sds((8, W), F32),
            sds((blocks, 6 * CB, 2 * CB), BF),
        ),
        in_specs=[any_spec, any_spec, any_spec, vmem, smem],
        out_specs=(any_spec, any_spec, vmem, vmem, any_spec),
        scratch_shapes=[
            pltpu.VMEM((rows, C), BF),
            pltpu.VMEM((C, W), BF),
            pltpu.VMEM((rows, W), F32),
            pltpu.VMEM((rows, W), F32),
            pltpu.VMEM((grp, taps_rows + 16, cg), BF),
            pltpu.VMEM((blocks, 6 * CB, 2 * CB), BF),
            pltpu.VMEM((blocks, 6 * CB, 2 * CB), BF),
            pltpu.VMEM((span, 3 * CB), BF),
            pltpu.VMEM((devices, 1, 128), F32),
            pltpu.VMEM((2, devices, 2, half), F32),
            pltpu.VMEM((2, devices, 2, half), F32),
            dma((5,)),
            dma((4,)),
            dma((2, grp - 1)),
            dma((2,)),
            dma((2, 2)),
            dma((2, 2)),
        ],
        compiler_params=params(0),
    )(x, conv_reduce, packed, par1, slot_mask)

    block_out, pre, ein, h2, sums3 = pl.pallas_call(
        functools.partial(kb_kernel, dims),
        name="middle_b",
        out_shape=(
            sds((rows, C), BF),
            sds((rows, C), F32),
            sds((rows, C), BF),
            sds((rows, W), BF),
            sds((2, C), F32),
        ),
        in_specs=[any_spec, vmem, any_spec, any_spec, any_spec, vmem, smem],
        out_specs=(any_spec, any_spec, any_spec, any_spec, vmem),
        scratch_shapes=[
            pltpu.VMEM((rows, W), F32),
            pltpu.VMEM((W, C), BF),
            pltpu.VMEM((rows, W), BF),
            pltpu.VMEM((rows, C), F32),
            pltpu.VMEM((rows, C), BF),
            pltpu.VMEM((rows, C), BF),
            pltpu.VMEM((rows, C), BF),
            pltpu.VMEM((8, C), F32),
            pltpu.VMEM((devices, 1, 128), F32),
            pltpu.VMEM((parts, devices, 2, 512), F32),
            pltpu.VMEM((parts, devices, 2, 512), F32),
            dma((10,)),
            dma((3 + parts,)),
            dma((2,)),
            dma((2, parts)),
            dma((2, parts)),
        ],
        compiler_params=params(1),
    )(mixed, p2, conv_expand, x, upstream, par3, slot_mask)

    flat = W * C // 128
    image_grad, rwg_sum, ewg_sum, gwg_sum, sums1, sums2 = pl.pallas_call(
        functools.partial(kc_kernel, dims),
        name="backward_c",
        out_shape=(
            sds((rows, C), BF),
            sds((flat, 128), BF),
            sds((flat, 128), BF),
            sds((tap_units * 16 * devices, 128), BF),
            sds((2, W), F32),
            sds((2, W), F32),
        ),
        in_specs=[any_spec] * 5 + [vmem] * 2 + [any_spec] * 4 + [smem],
        out_specs=(any_spec, any_spec, any_spec, any_spec, vmem, vmem),
        scratch_shapes=[
            pltpu.VMEM((rows, W), BF),
            pltpu.VMEM((rows, W), BF),
            pltpu.VMEM((rows, W), F32),
            pltpu.VMEM((rows, W), F32),
            pltpu.VMEM((rows, C), BF),
            pltpu.VMEM((C // W, W, W), BF),
            pltpu.VMEM((2, rows // 2, 512), F32),
            pltpu.VMEM((flat, 128), BF),
            pltpu.VMEM((flat, 128), BF),
            pltpu.VMEM((flat, 128), BF),
            pltpu.VMEM((flat, 128), BF),
            pltpu.VMEM((tap_units * 16 * devices, 128), BF),
            pltpu.VMEM((tap_units * 16 * devices, 128), BF),
            pltpu.VMEM((2, 6 * CB, 2 * CB), BF),
            pltpu.VMEM((span, 3 * CB), BF),
            pltpu.VMEM((span, CB), BF),
            pltpu.VMEM((8, W), F32),
            pltpu.VMEM((2, devices, 2, half), F32),
            pltpu.VMEM((2, devices, 2, half), F32),
            dma((16,)),
            dma((2,)),
            dma((2,)),
            dma((parts,)),
            dma((2, 2)),
            dma((2, 2)),
            dma((2, 2, 3, stages)),
            dma((2, 2, 3, stages)),
            dma((2, 3, stages)),
            dma((5, 3)),
        ],
        compiler_params=params(2),
    )(mixed, red, ein, h2, conv_expand, p1, p2, back, x, conv_reduce, pre, slot_mask)

    reduce_wgrad, expand_wgrad = wgrad_results(rwg_sum, ewg_sum, C, W)
    shard = cg // CB
    gwg_sum = gwg_sum[: taps_rows * blocks].reshape(blocks, taps_rows, CB)
    gwg_sum = lax.dynamic_slice_in_dim(gwg_sum, lax.axis_index("grp") * shard, shard, 0)
    group_wgrad = columns_last(gwg_sum)
    own = lax.dynamic_slice_in_dim(sums2, lax.axis_index("grp") * cg, cg, 1)
    return (
        images_first(block_out, n, side),
        images_first(image_grad, n, side),
        reduce_wgrad,
        sums1[0],
        sums1[1],
        group_wgrad.reshape(conv_group.shape),
        own[0],
        own[1],
        expand_wgrad,
        sums3[0],
        sums3[1],
    )


def solution(mesh):
    placed = (
        P(("grp", "dp"), None, None, None),
        P(("grp", "dp")),
        P(),
        P(),
        P(),
        P(None, None, None, "grp"),
        P("grp"),
        P("grp"),
        P(),
        P(),
        P(),
        P(("grp", "dp"), None, None, None),
    )
    return jax.shard_map(
        functools.partial(per_device, mesh.shape["grp"], mesh.shape["dp"]),
        mesh=mesh,
        in_specs=placed,
        out_specs=(
            P(("grp", "dp"), None, None, None),
            P(("grp", "dp"), None, None, None),
            P(),
            P(),
            P(),
            P(None, None, None, "grp"),
            P("grp"),
            P("grp"),
            P(),
            P(),
            P(),
        ),
        check_vma=False,
    )
```
